256 devices in a mesh: gx: 8 (over z_hi, y), gy: 32 (over x, z_lo, core).
Axes of the slice: x: 4, y: 4, z: 8 (z_hi: 2, z_lo: 4; z = z_hi * 4 + z_lo), core: 2. Of those that a mesh axis runs over, the one named last changes fastest.
Arguments:
- density: float32 [2, 2048, 8192], P(None, 'gx', 'gy'), may hold values from -6 to 6
- observed: float32 [2048, 8192], P('gx', 'gy'), may hold values from -6 to 6
- stations: int32 [2048, 8192], P('gx', 'gy'), may hold values 0 or 1
- layer_index: int32 [2], replicated, may hold values from 0 to 511
Outputs:
- predicted: float32 [2048, 8192], P('gx', 'gy')
- residual: float32 [2048, 8192], P('gx', 'gy')
- gradient: float32 [2, 2048, 8192], P(None, 'gx', 'gy')
The draws below stay inside these ranges and needn't reach their ends.
All inputs are finite; a program needn't handle non-finite values. No bound on the sum of `stations` on one device may be relied on, other than what follows from the above.
Results may differ from the reference program's by a relative error of at most 0.00016.
Values sent between devices are 32-bit elements; how exact they have to be, the bound alone decides.
A program may use at most 64 MiB of HBM per device.

```python
import jax
import jax.numpy as jnp

LAYERS = 2
RADIUS = 128
LAYERS_ALL = 512
NX = 2048
NY = 8192


def with_ends(array, own_key, smallest, largest):
    index_at = [jax.random.randint(jax.random.fold_in(own_key, axis), (), 0, length) for axis, length in enumerate(array.shape)]
    longest = array.shape.index(max(array.shape))
    beside = index_at[:longest] + [(index_at[longest] + 1) % array.shape[longest]] + index_at[longest + 1:]
    return array.at[tuple(index_at)].set(smallest).at[tuple(beside)].set(largest)


def level_of(own_key, dims, cuts, least, top_value):
    def one(dim, blocks):
        heights = jax.random.uniform(jax.random.fold_in(jax.random.fold_in(own_key, 6), dim), (blocks,), jnp.float32, least / len(cuts), top_value / len(cuts))
        return jnp.repeat(jnp.exp(heights), dims[dim] // blocks).reshape((-1,) + (1,) * (len(dims) - dim - 1))

    gain = one(*cuts[0])
    for cut in cuts[1:]:
        gain = gain * one(*cut)
    return gain


def centred(rng, shape, deviation, bound, cuts=(), held_as=jnp.bfloat16):
    loudness = level_of(rng, shape, cuts, -0.22, 0.18) if cuts else 1.0
    array = jax.random.normal(rng, shape, jnp.float32) * deviation * loudness
    return jnp.minimum(jnp.maximum(array, -bound), bound).astype(held_as)


def setup_inputs(seed: int = 0) -> dict:
    key_list = jax.random.split(jax.random.key(seed), 5)
    density = centred(key_list[0], (LAYERS, NX, NY), 1.0, 6.0, ((1, 8), (2, 32)), jnp.float32)
    observed = centred(key_list[1], (NX, NY), 1.0, 6.0, ((0, 8), (1, 32)), jnp.float32)
    stations = with_ends((jax.random.randint(key_list[2], (NX, NY), 0, 2) < 1).astype(jnp.int32), jax.random.fold_in(key_list[2], 1), 0, 1)
    layer_index = jax.random.randint(key_list[3], (LAYERS,), 0, LAYERS_ALL).astype(jnp.int32)
    return {"density": density, "observed": observed, "stations": stations, "layer_index": layer_index}


def signed_offsets(length):
    ticks = jnp.arange(length, dtype=jnp.int32)
    return jnp.where(ticks <= RADIUS, ticks, ticks - length).astype(jnp.float32)

def kernel_grid(index, rows, cols):
    first = signed_offsets(rows)
    second = signed_offsets(cols)
    depth = RADIUS * (0.375 + index.astype(jnp.float32) / LAYERS_ALL)
    square = first[:, None] ** 2 + second[None, :] ** 2 + depth * depth
    value = depth * depth / (square * jnp.sqrt(square))
    inside = (jnp.abs(first) <= RADIUS)[:, None] & (jnp.abs(second) <= RADIUS)[None, :]
    return jnp.where(inside, value, jnp.zeros_like(value))

def convolve(kernel_hat, field, rows, cols):
    padded = jnp.pad(field, RADIUS)
    whole = jnp.fft.irfft2(kernel_hat * jnp.fft.rfft2(padded), s=(rows, cols))
    return whole[RADIUS:RADIUS + NX, RADIUS:RADIUS + NY].astype(jnp.float32)

def reference(density, observed, stations, layer_index):
    rows = NX + 2 * RADIUS
    cols = NY + 2 * RADIUS
    spectra = [jnp.fft.rfft2(kernel_grid(layer_index[layer], rows, cols)) for layer in range(LAYERS)]
    predicted = jnp.zeros((NX, NY), jnp.float32)
    for layer in range(LAYERS):
        predicted = predicted + convolve(spectra[layer], density[layer], rows, cols)
    residual = stations.astype(jnp.float32) * (predicted - observed)
    gradient = jnp.stack([convolve(spectra[layer], residual, rows, cols) for layer in range(LAYERS)])
    return (predicted, residual, gradient)
```

```python
import functools
import math

import jax
import jax.numpy as jnp
import numpy as np
from jax import lax
from jax.experimental import pallas as pl
from jax.experimental.pallas import tpu as pltpu
from jax.sharding import PartitionSpec as P

RADIUS = 128
LAYERS_ALL = 512
MESH = pl.DeviceIdType.MESH
F32 = jnp.float32
BF16 = jnp.bfloat16

DIRS = ((1, 0), (-1, 0), (1, 1), (1, -1), (-1, 1), (-1, -1), (0, 1), (0, -1))


def halves(table):
    high = table.astype(BF16)
    return high, (table - high.astype(np.float64)).astype(BF16)


def tables(length):
    half = length // 2
    odd = 2 * np.arange(half)[:, None] + 1
    phase = (odd * (2 * np.arange(length)[None, :] - length + 1)) % (4 * length)
    angle = phase * (2.0 * math.pi / (4 * length))
    basis = np.concatenate([np.cos(angle), np.sin(angle)])
    ticks = np.arange(half)[None, :]
    kphase = (odd * ticks) % (2 * length)
    weight = np.where(ticks == 0, 1.0, 2.0) * (ticks <= RADIUS) / half
    cosines = np.cos(kphase * (2.0 * math.pi / (2 * length))) * weight
    return halves(basis), halves(np.ascontiguousarray(basis.T)), halves(cosines)


def dot(left, right):
    return lax.dot_general(left, right, (((1,), (0,)), ((), ())), preferred_element_type=F32)


def dot_t(left, right):
    return lax.dot_general(left, right, (((1,), (1,)), ((), ())), preferred_element_type=F32)


def split(value):
    high = value.astype(BF16)
    return high, (value - high.astype(F32)).astype(BF16)


def product(left, right, how=dot):
    return how(left[0], right[0]) + (how(left[1], right[0]) + how(left[0], right[1]))


def part(refs, rows, cols):
    return refs[0][rows, cols], refs[1][rows, cols]


def put(refs, rows, cols, value):
    refs[0][rows, cols], refs[1][rows, cols] = split(value)


def forward_kernel(
    counts,
    index, density, observed, stations, bas_h, bas_l, tra_h, tra_l, cos_h, cos_l,
    predicted, residual, blocks, spectra,
    den, obs, sta, b_h, b_l, t_h, t_l, c_h, c_l,
    s_h, s_l, z_h, z_l, total, big, win, from_x, from_y, from_d,
    load_sem, send_sem, recv_sem,
):
    gx, gy = lax.axis_index("gx"), lax.axis_index("gy")
    nx, ny = counts
    layers, tile = den.shape[0], den.shape[1]
    length = tile + 2 * RADIUS
    half = length // 2
    low, mid, high = slice(0, RADIUS), slice(RADIUS, RADIUS + tile), slice(RADIUS + tile, length)
    first, last = slice(RADIUS, 2 * RADIUS), slice(tile, RADIUS + tile)
    every = slice(0, length)

    def there(dx, dy):
        conds = []
        if dx:
            conds.append(gx < nx - 1 if dx > 0 else gx > 0)
        if dy:
            conds.append(gy < ny - 1 if dy > 0 else gy > 0)
        return functools.reduce(jnp.logical_and, conds)

    def target(dx, dy):
        return {"gx": gx + dx, "gy": gy + dy}

    barrier = pltpu.get_barrier_semaphore()
    for dx, dy in DIRS:
        @pl.when(there(dx, dy))
        def _(dx=dx, dy=dy):
            pl.semaphore_signal(barrier, inc=1, device_id=target(dx, dy), device_id_type=MESH)

    pairs = ((cos_h, c_h), (cos_l, c_l), (density, den), (tra_h, t_h), (tra_l, t_l), (bas_h, b_h), (bas_l, b_l), (observed, obs), (stations, sta))
    loads = [pltpu.make_async_copy(src, dst, load_sem.at[i]) for i, (src, dst) in enumerate(pairs)]
    for load in loads:
        load.start()

    @pl.when(gx == 0)
    def _():
        win[low, :] = jnp.zeros((RADIUS, length), F32)

    @pl.when(gx == nx - 1)
    def _():
        win[high, :] = jnp.zeros((RADIUS, length), F32)

    @pl.when(gy == 0)
    def _():
        win[:, low] = jnp.zeros((length, RADIUS), F32)

    @pl.when(gy == ny - 1)
    def _():
        win[:, high] = jnp.zeros((length, RADIUS), F32)

    rows = lax.broadcasted_iota(jnp.int32, (half, half), 0).astype(F32)
    cols = lax.broadcasted_iota(jnp.int32, (half, half), 1).astype(F32)
    flat = rows * rows + cols * cols
    loads[0].wait()
    loads[1].wait()
    cosines = (c_h[...], c_l[...])
    for layer in range(layers):
        depth = RADIUS * (0.375 + index[layer].astype(F32) / LAYERS_ALL)
        square = flat + depth * depth
        inverse = lax.rsqrt(square)
        value = (depth * depth) * (inverse * inverse * inverse)
        left = product(cosines, split(value))
        spectra[layer] = product(split(left), cosines, dot_t)

    for load in loads[2:7]:
        load.wait()
    basis, trans = (b_h, b_l), (t_h, t_l)
    for layer in range(layers):
        put((s_h, s_l), slice(0, tile), every, product(split(den[layer]), part(trans, mid, every)))
        spectrum = spectra[layer]
        for r in range(2):
            band = slice(r * half, (r + 1) * half)
            out = product(part(basis, band, mid), part((s_h, s_l), slice(0, tile), every))
            for c in range(2):
                at = slice(c * half, (c + 1) * half)
                term = spectrum * out[:, at]
                total[band, at] = term if layer == 0 else total[band, at] + term
    for r in range(2):
        band = slice(r * half, (r + 1) * half)
        put((z_h, z_l), band, every, total[band, :])
    for r in range(2):
        band = slice(r * half, (r + 1) * half)
        put((s_h, s_l), band, every, product(part((z_h, z_l), band, every), part(basis, every, every)))

    def pieces(dx, dy):
        rs = {1: high, -1: low, 0: mid}[dx]
        cs = {1: high, -1: low, 0: mid}[dy]
        if dx and dy:
            return big.at[rs, cs], from_d.at[(dx < 0) * 2 + (dy < 0)]
        if dx:
            return big.at[rs, cs], from_x.at[int(dx < 0)]
        return big.at[rs, cs], from_y.at[int(dy < 0)]

    def fold_copy(k):
        dx, dy = DIRS[k]
        src, dst = pieces(dx, dy)
        return pltpu.make_async_remote_copy(
            src_ref=src, dst_ref=dst, send_sem=send_sem.at[0, k], recv_sem=recv_sem.at[0, k],
            device_id=target(dx, dy), device_id_type=MESH,
        )

    def halo_copy(k):
        dx, dy = DIRS[k]
        near, far = {1: last, -1: first, 0: mid}, {1: low, -1: high, 0: mid}
        return pltpu.make_async_remote_copy(
            src_ref=win.at[near[dx], near[dy]], dst_ref=win.at[far[dx], far[dy]],
            send_sem=send_sem.at[1, k], recv_sem=recv_sem.at[1, k],
            device_id=target(dx, dy), device_id_type=MESH,
        )

    def start(make, ks):
        for k in ks:
            @pl.when(there(*DIRS[k]))
            def _(k=k):
                make(k).start()

    def sent(make):
        for k in range(8):
            @pl.when(there(*DIRS[k]))
            def _(k=k):
                make(k).wait_send()

    def received(make, ks, then=None):
        for k in ks:
            dx, dy = DIRS[k]
            @pl.when(there(-dx, -dy))
            def _(k=k):
                make(k).wait_recv()
                if then is not None:
                    then(k)

    sides_x = 2 - (gx == 0).astype(jnp.int32) - (gx == nx - 1).astype(jnp.int32)
    sides_y = 2 - (gy == 0).astype(jnp.int32) - (gy == ny - 1).astype(jnp.int32)
    pl.semaphore_wait(barrier, (sides_x + 1) * (sides_y + 1) - 1)

    def back(rs, cs):
        big[rs, cs] = product(part(trans, rs, every), part((s_h, s_l), every, cs))

    back(high, every)
    start(fold_copy, (0, 2, 3))
    back(low, every)
    start(fold_copy, (1, 4, 5))
    back(mid, every)
    start(fold_copy, (6, 7))
    for load in loads[7:]:
        load.wait()

    def fold(k):
        dx, dy = DIRS[k]
        rs = {1: first, -1: last, 0: mid}[dx]
        cs = {1: first, -1: last, 0: mid}[dy]
        big[rs, cs] = big[rs, cs] + pieces(dx, dy)[1][...]

    received(fold_copy, (6, 7, 0, 1, 2, 3, 4, 5), fold)
    total_pred = big[mid, mid]
    misfit = sta[...].astype(F32) * (total_pred - obs[...])
    win[mid, mid] = misfit
    start(halo_copy, range(8))
    predicted[...] = total_pred
    residual[...] = misfit

    received(halo_copy, (6, 7))
    put((s_h, s_l), slice(0, tile), every, product(split(win[mid, :]), part(trans, every, every)))
    for r in range(2):
        band = slice(r * half, (r + 1) * half)
        total[band, :] = product(part(basis, band, mid), part((s_h, s_l), slice(0, tile), every))

    received(halo_copy, range(6))
    put((s_h, s_l), low, every, product(split(win[low, :]), part(trans, every, every)))
    put((s_h, s_l), high, every, product(split(win[high, :]), part(trans, every, every)))
    for r in range(2):
        band = slice(r * half, (r + 1) * half)
        blocks[band, :] = (
            total[band, :]
            + product(part(basis, band, low), part((s_h, s_l), low, every))
            + product(part(basis, band, high), part((s_h, s_l), high, every))
        )
    sent(fold_copy)
    sent(halo_copy)


def adjoint_kernel(
    predicted, residual, blocks, spectra, bas_h, bas_l, tra_h, tra_l,
    predicted_out, residual_out, gradient,
    b_h, b_l, t_h, t_l, z_h, z_l, w_h, w_l, grad, load_sem, out_sem,
):
    layers, tile = spectra.shape[0], residual.shape[0]
    length = tile + 2 * RADIUS
    half = length // 2
    mid = slice(RADIUS, RADIUS + tile)
    every = slice(0, length)
    loads = [
        pltpu.make_async_copy(bas_h.at[:, mid], b_h, load_sem.at[0]),
        pltpu.make_async_copy(bas_l.at[:, mid], b_l, load_sem.at[1]),
        pltpu.make_async_copy(tra_h.at[mid, :], t_h, load_sem.at[2]),
        pltpu.make_async_copy(tra_l.at[mid, :], t_l, load_sem.at[3]),
    ]
    for load in loads:
        load.start()
    stores = [
        pltpu.make_async_copy(predicted, predicted_out, out_sem.at[0]),
        pltpu.make_async_copy(residual, residual_out, out_sem.at[1]),
    ]
    for store in stores:
        store.start()
    for load in loads:
        load.wait()
    for layer in range(layers):
        spectrum = spectra[layer]
        for r in range(2):
            band = slice(r * half, (r + 1) * half)
            for c in range(2):
                at = slice(c * half, (c + 1) * half)
                put((z_h, z_l), band, at, spectrum * blocks[band, at])
        for r in range(2):
            band = slice(r * half, (r + 1) * half)
            put((w_h, w_l), band, slice(0, tile), product(part((z_h, z_l), band, every), (b_h[...], b_l[...])))
        grad[layer] = product((t_h[...], t_l[...]), (w_h[...], w_l[...]))
        store = pltpu.make_async_copy(grad.at[layer], gradient.at[layer], out_sem.at[2 + layer])
        store.start()
        stores.append(store)
    for store in stores:
        store.wait()


def solution(mesh):
    counts = (mesh.shape["gx"], mesh.shape["gy"])

    def body(density, observed, stations, layer_index):
        layers, tile = density.shape[0], density.shape[1]
        length = tile + 2 * RADIUS
        half = length // 2
        (bas_h, bas_l), (tra_h, tra_l), (cos_h, cos_l) = tables(length)
        anywhere = pl.BlockSpec(memory_space=pl.ANY)
        vmem = pl.BlockSpec(memory_space=pltpu.VMEM)
        big = pltpu.VMEM((length, length), F32)
        wide = pltpu.VMEM((length, length), BF16)
        small = pltpu.VMEM((half, half), BF16)
        predicted, residual, blocks, spectra = pl.pallas_call(
            functools.partial(forward_kernel, counts),
            out_shape=(
                pltpu.VMEM((tile, tile), F32),
                pltpu.VMEM((tile, tile), F32),
                pltpu.VMEM((length, length), F32),
                pltpu.VMEM((layers, half, half), F32),
            ),
            in_specs=[pl.BlockSpec(memory_space=pltpu.SMEM)] + [anywhere] * 9,
            out_specs=(vmem,) * 4,
            scratch_shapes=[
                pltpu.VMEM(density.shape, F32),
                pltpu.VMEM((tile, tile), F32),
                pltpu.VMEM((tile, tile), jnp.int32),
                wide, wide, wide, wide, small, small,
                wide, wide, wide, wide, big, big, big,
                pltpu.VMEM((2, RADIUS, tile), F32),
                pltpu.VMEM((2, tile, RADIUS), F32),
                pltpu.VMEM((4, RADIUS, RADIUS), F32),
                pltpu.SemaphoreType.DMA((9,)),
                pltpu.SemaphoreType.DMA((2, 8)),
                pltpu.SemaphoreType.DMA((2, 8)),
            ],
            compiler_params=pltpu.CompilerParams(
                collective_id=0, has_side_effects=True, vmem_limit_bytes=32 << 20
            ),
            name="forward",
        )(layer_index, density, observed, stations, bas_h, bas_l, tra_h, tra_l, cos_h, cos_l)
        return pl.pallas_call(
            adjoint_kernel,
            out_shape=(
                jax.ShapeDtypeStruct((tile, tile), F32),
                jax.ShapeDtypeStruct((tile, tile), F32),
                jax.ShapeDtypeStruct((layers, tile, tile), F32),
            ),
            in_specs=[vmem] * 4 + [anywhere] * 4,
            out_specs=(anywhere,) * 3,
            scratch_shapes=[
                pltpu.VMEM((length, tile), BF16),
                pltpu.VMEM((length, tile), BF16),
                pltpu.VMEM((tile, length), BF16),
                pltpu.VMEM((tile, length), BF16),
                wide, wide,
                pltpu.VMEM((length, tile), BF16),
                pltpu.VMEM((length, tile), BF16),
                pltpu.VMEM((layers, tile, tile), F32),
                pltpu.SemaphoreType.DMA((4,)),
                pltpu.SemaphoreType.DMA((2 + layers,)),
            ],
            compiler_params=pltpu.CompilerParams(vmem_limit_bytes=24 << 20),
            name="adjoint",
        )(predicted, residual, blocks, spectra, bas_h, bas_l, tra_h, tra_l)

    in_specs = (P(None, "gx", "gy"), P("gx", "gy"), P("gx", "gy"), P())
    out_specs = (P("gx", "gy"), P("gx", "gy"), P(None, "gx", "gy"))
    return jax.shard_map(body, mesh=mesh, in_specs=in_specs, out_specs=out_specs, check_vma=False)
```

```python
import functools
import math

import jax
import jax.numpy as jnp
import numpy as np
from jax import lax
from jax.experimental import pallas as pl
from jax.experimental.pallas import tpu as pltpu
from jax.sharding import PartitionSpec as P

RADIUS = 128
LAYERS_ALL = 512
MESH = pl.DeviceIdType.MESH
F32 = jnp.float32
BF16 = jnp.bfloat16

DIRS = ((1, 0), (-1, 0), (1, 1), (1, -1), (-1, 1), (-1, -1), (0, 1), (0, -1))


def halves(table):
    high = table.astype(BF16)
    return high, (table - high.astype(np.float64)).astype(BF16)


def tables(length):
    half = length // 2
    odd = 2 * np.arange(half)[:, None] + 1
    phase = (odd * (2 * np.arange(length)[None, :] - length + 1)) % (4 * length)
    angle = phase * (2.0 * math.pi / (4 * length))
    basis = np.concatenate([np.cos(angle), np.sin(angle)])
    ticks = np.arange(half)[None, :]
    kphase = (odd * ticks) % (2 * length)
    weight = np.where(ticks == 0, 1.0, 2.0) * (ticks <= RADIUS) / half
    cosines = np.cos(kphase * (2.0 * math.pi / (2 * length))) * weight
    return halves(basis), halves(np.ascontiguousarray(basis.T)), halves(cosines)


def dot(left, right):
    return lax.dot_general(left, right, (((1,), (0,)), ((), ())), preferred_element_type=F32)


def dot_t(left, right):
    return lax.dot_general(left, right, (((1,), (1,)), ((), ())), preferred_element_type=F32)


def in_hbm(array):
    return pltpu.with_memory_space_constraint(array, pltpu.HBM)


def split(value):
    high = value.astype(BF16)
    return high, (value - high.astype(F32)).astype(BF16)


def product(left, right, how=dot):
    return how(left[0], right[0]) + (how(left[1], right[0]) + how(left[0], right[1]))


def part(refs, rows, cols):
    return refs[0][rows, cols], refs[1][rows, cols]


def put(refs, rows, cols, value):
    refs[0][rows, cols], refs[1][rows, cols] = split(value)


def forward_kernel(
    counts,
    layer_index, density, observed, stations, bas_h, bas_l, tra_h, tra_l, cos_h, cos_l,
    predicted, residual, blocks, spectra,
    den, obs, sta, b_h, b_l, t_h, t_l, c_h, c_l,
    s_h, s_l, z_h, z_l, total, big, win, from_x, from_y, from_d,
    index, index_sem, load_sem, send_sem, recv_sem,
):
    gx, gy = lax.axis_index("gx"), lax.axis_index("gy")
    nx, ny = counts
    layers, tile = den.shape[0], den.shape[1]
    length = tile + 2 * RADIUS
    half = length // 2
    low, mid, high = slice(0, RADIUS), slice(RADIUS, RADIUS + tile), slice(RADIUS + tile, length)
    first, last = slice(RADIUS, 2 * RADIUS), slice(tile, RADIUS + tile)
    every = slice(0, length)

    def there(dx, dy):
        conds = []
        if dx:
            conds.append(gx < nx - 1 if dx > 0 else gx > 0)
        if dy:
            conds.append(gy < ny - 1 if dy > 0 else gy > 0)
        return functools.reduce(jnp.logical_and, conds)

    def target(dx, dy):
        return {"gx": gx + dx, "gy": gy + dy}

    barrier = pltpu.get_barrier_semaphore()
    for dx, dy in DIRS:
        @pl.when(there(dx, dy))
        def _(dx=dx, dy=dy):
            pl.semaphore_signal(barrier, inc=1, device_id=target(dx, dy), device_id_type=MESH)

    pairs = ((cos_h, c_h), (cos_l, c_l), (density, den), (tra_h, t_h), (tra_l, t_l), (bas_h, b_h), (bas_l, b_l), (observed, obs), (stations, sta))
    loads = [pltpu.make_async_copy(src, dst, load_sem.at[i]) for i, (src, dst) in enumerate(pairs)]
    index_load = pltpu.make_async_copy(layer_index, index, index_sem)
    index_load.start()
    for load in loads:
        load.start()

    @pl.when(gx == 0)
    def _():
        win[low, :] = jnp.zeros((RADIUS, length), F32)

    @pl.when(gx == nx - 1)
    def _():
        win[high, :] = jnp.zeros((RADIUS, length), F32)

    @pl.when(gy == 0)
    def _():
        win[:, low] = jnp.zeros((length, RADIUS), F32)

    @pl.when(gy == ny - 1)
    def _():
        win[:, high] = jnp.zeros((length, RADIUS), F32)

    rows = lax.broadcasted_iota(jnp.int32, (half, half), 0).astype(F32)
    cols = lax.broadcasted_iota(jnp.int32, (half, half), 1).astype(F32)
    flat = rows * rows + cols * cols
    index_load.wait()
    loads[0].wait()
    loads[1].wait()
    cosines = (c_h[...], c_l[...])
    for layer in range(layers):
        depth = RADIUS * (0.375 + index[layer].astype(F32) / LAYERS_ALL)
        square = flat + depth * depth
        inverse = lax.rsqrt(square)
        value = (depth * depth) * (inverse * inverse * inverse)
        left = product(cosines, split(value))
        spectra[layer] = product(split(left), cosines, dot_t)

    for load in loads[2:7]:
        load.wait()
    basis, trans = (b_h, b_l), (t_h, t_l)
    for layer in range(layers):
        put((s_h, s_l), slice(0, tile), every, product(split(den[layer]), part(trans, mid, every)))
        spectrum = spectra[layer]
        for r in range(2):
            band = slice(r * half, (r + 1) * half)
            out = product(part(basis, band, mid), part((s_h, s_l), slice(0, tile), every))
            for c in range(2):
                at = slice(c * half, (c + 1) * half)
                term = spectrum * out[:, at]
                total[band, at] = term if layer == 0 else total[band, at] + term
    for r in range(2):
        band = slice(r * half, (r + 1) * half)
        put((z_h, z_l), band, every, total[band, :])
    for r in range(2):
        band = slice(r * half, (r + 1) * half)
        put((s_h, s_l), band, every, product(part((z_h, z_l), band, every), part(basis, every, every)))

    def pieces(dx, dy):
        rs = {1: high, -1: low, 0: mid}[dx]
        cs = {1: high, -1: low, 0: mid}[dy]
        if dx and dy:
            return big.at[rs, cs], from_d.at[(dx < 0) * 2 + (dy < 0)]
        if dx:
            return big.at[rs, cs], from_x.at[int(dx < 0)]
        return big.at[rs, cs], from_y.at[int(dy < 0)]

    def fold_copy(k):
        dx, dy = DIRS[k]
        src, dst = pieces(dx, dy)
        return pltpu.make_async_remote_copy(
            src_ref=src, dst_ref=dst, send_sem=send_sem.at[0, k], recv_sem=recv_sem.at[0, k],
            device_id=target(dx, dy), device_id_type=MESH,
        )

    def halo_copy(k):
        dx, dy = DIRS[k]
        near, far = {1: last, -1: first, 0: mid}, {1: low, -1: high, 0: mid}
        return pltpu.make_async_remote_copy(
            src_ref=win.at[near[dx], near[dy]], dst_ref=win.at[far[dx], far[dy]],
            send_sem=send_sem.at[1, k], recv_sem=recv_sem.at[1, k],
            device_id=target(dx, dy), device_id_type=MESH,
        )

    def start(make, ks):
        for k in ks:
            @pl.when(there(*DIRS[k]))
            def _(k=k):
                make(k).start()

    def sent(make):
        for k in range(8):
            @pl.when(there(*DIRS[k]))
            def _(k=k):
                make(k).wait_send()

    def received(make, ks, then=None):
        for k in ks:
            dx, dy = DIRS[k]
            @pl.when(there(-dx, -dy))
            def _(k=k):
                make(k).wait_recv()
                if then is not None:
                    then(k)

    sides_x = 2 - (gx == 0).astype(jnp.int32) - (gx == nx - 1).astype(jnp.int32)
    sides_y = 2 - (gy == 0).astype(jnp.int32) - (gy == ny - 1).astype(jnp.int32)
    pl.semaphore_wait(barrier, (sides_x + 1) * (sides_y + 1) - 1)

    def back(rs, cs):
        big[rs, cs] = product(part(trans, rs, every), part((s_h, s_l), every, cs))

    back(high, every)
    start(fold_copy, (0, 2, 3))
    back(low, every)
    start(fold_copy, (1, 4, 5))
    back(mid, every)
    start(fold_copy, (6, 7))
    for load in loads[7:]:
        load.wait()

    def fold(k):
        dx, dy = DIRS[k]
        rs = {1: first, -1: last, 0: mid}[dx]
        cs = {1: first, -1: last, 0: mid}[dy]
        big[rs, cs] = big[rs, cs] + pieces(dx, dy)[1][...]

    received(fold_copy, (6, 7, 0, 1, 2, 3, 4, 5), fold)
    total_pred = big[mid, mid]
    misfit = sta[...].astype(F32) * (total_pred - obs[...])
    win[mid, mid] = misfit
    start(halo_copy, range(8))
    predicted[...] = total_pred
    residual[...] = misfit

    received(halo_copy, (6, 7))
    put((s_h, s_l), slice(0, tile), every, product(split(win[mid, :]), part(trans, every, every)))
    for r in range(2):
        band = slice(r * half, (r + 1) * half)
        total[band, :] = product(part(basis, band, mid), part((s_h, s_l), slice(0, tile), every))

    received(halo_copy, range(6))
    put((s_h, s_l), low, every, product(split(win[low, :]), part(trans, every, every)))
    put((s_h, s_l), high, every, product(split(win[high, :]), part(trans, every, every)))
    for r in range(2):
        band = slice(r * half, (r + 1) * half)
        blocks[band, :] = (
            total[band, :]
            + product(part(basis, band, low), part((s_h, s_l), low, every))
            + product(part(basis, band, high), part((s_h, s_l), high, every))
        )
    sent(fold_copy)
    sent(halo_copy)


def adjoint_kernel(
    predicted, residual, blocks, spectra, bas_h, bas_l, tra_h, tra_l,
    predicted_out, residual_out, gradient,
    b_h, b_l, t_h, t_l, z_h, z_l, w_h, w_l, grad, load_sem, out_sem,
):
    layers, tile = spectra.shape[0], residual.shape[0]
    length = tile + 2 * RADIUS
    half = length // 2
    mid = slice(RADIUS, RADIUS + tile)
    every = slice(0, length)
    loads = [
        pltpu.make_async_copy(bas_h.at[:, mid], b_h, load_sem.at[0]),
        pltpu.make_async_copy(bas_l.at[:, mid], b_l, load_sem.at[1]),
        pltpu.make_async_copy(tra_h.at[mid, :], t_h, load_sem.at[2]),
        pltpu.make_async_copy(tra_l.at[mid, :], t_l, load_sem.at[3]),
    ]
    for load in loads:
        load.start()
    stores = [
        pltpu.make_async_copy(predicted, predicted_out, out_sem.at[0]),
        pltpu.make_async_copy(residual, residual_out, out_sem.at[1]),
    ]
    for store in stores:
        store.start()
    for load in loads:
        load.wait()
    for layer in range(layers):
        spectrum = spectra[layer]
        for r in range(2):
            band = slice(r * half, (r + 1) * half)
            for c in range(2):
                at = slice(c * half, (c + 1) * half)
                put((z_h, z_l), band, at, spectrum * blocks[band, at])
        for r in range(2):
            band = slice(r * half, (r + 1) * half)
            put((w_h, w_l), band, slice(0, tile), product(part((z_h, z_l), band, every), (b_h[...], b_l[...])))
        grad[layer] = product((t_h[...], t_l[...]), (w_h[...], w_l[...]))
        store = pltpu.make_async_copy(grad.at[layer], gradient.at[layer], out_sem.at[2 + layer])
        store.start()
        stores.append(store)
    for store in stores:
        store.wait()


def solution(mesh):
    counts = (mesh.shape["gx"], mesh.shape["gy"])

    def body(density, observed, stations, layer_index):
        layers, tile = density.shape[0], density.shape[1]
        length = tile + 2 * RADIUS
        half = length // 2
        (bas_h, bas_l), (tra_h, tra_l), (cos_h, cos_l) = tables(length)
        anywhere = pl.BlockSpec(memory_space=pl.ANY)
        vmem = pl.BlockSpec(memory_space=pltpu.VMEM)
        big = pltpu.VMEM((length, length), F32)
        wide = pltpu.VMEM((length, length), BF16)
        small = pltpu.VMEM((half, half), BF16)
        predicted, residual, blocks, spectra = pl.pallas_call(
            functools.partial(forward_kernel, counts),
            out_shape=(
                pltpu.VMEM((tile, tile), F32),
                pltpu.VMEM((tile, tile), F32),
                pltpu.VMEM((length, length), F32),
                pltpu.VMEM((layers, half, half), F32),
            ),
            in_specs=[anywhere] * 10,
            out_specs=(vmem,) * 4,
            scratch_shapes=[
                pltpu.VMEM(density.shape, F32),
                pltpu.VMEM((tile, tile), F32),
                pltpu.VMEM((tile, tile), jnp.int32),
                wide, wide, wide, wide, small, small,
                wide, wide, wide, wide, big, big, big,
                pltpu.VMEM((2, RADIUS, tile), F32),
                pltpu.VMEM((2, tile, RADIUS), F32),
                pltpu.VMEM((4, RADIUS, RADIUS), F32),
                pltpu.SMEM((layers,), jnp.int32),
                pltpu.SemaphoreType.DMA,
                pltpu.SemaphoreType.DMA((9,)),
                pltpu.SemaphoreType.DMA((2, 8)),
                pltpu.SemaphoreType.DMA((2, 8)),
            ],
            compiler_params=pltpu.CompilerParams(
                collective_id=0, has_side_effects=True, vmem_limit_bytes=32 << 20
            ),
            name="forward",
        )(*map(in_hbm, (layer_index, density, observed, stations, bas_h, bas_l, tra_h, tra_l, cos_h, cos_l)))
        return pl.pallas_call(
            adjoint_kernel,
            out_shape=(
                jax.ShapeDtypeStruct((tile, tile), F32),
                jax.ShapeDtypeStruct((tile, tile), F32),
                jax.ShapeDtypeStruct((layers, tile, tile), F32),
            ),
            in_specs=[vmem] * 4 + [anywhere] * 4,
            out_specs=(anywhere,) * 3,
            scratch_shapes=[
                pltpu.VMEM((length, tile), BF16),
                pltpu.VMEM((length, tile), BF16),
                pltpu.VMEM((tile, length), BF16),
                pltpu.VMEM((tile, length), BF16),
                wide, wide,
                pltpu.VMEM((length, tile), BF16),
                pltpu.VMEM((length, tile), BF16),
                pltpu.VMEM((layers, tile, tile), F32),
                pltpu.SemaphoreType.DMA((4,)),
                pltpu.SemaphoreType.DMA((2 + layers,)),
            ],
            compiler_params=pltpu.CompilerParams(vmem_limit_bytes=24 << 20),
            name="adjoint",
        )(predicted, residual, blocks, spectra, *map(in_hbm, (bas_h, bas_l, tra_h, tra_l)))

    in_specs = (P(None, "gx", "gy"), P("gx", "gy"), P("gx", "gy"), P())
    out_specs = (P("gx", "gy"), P("gx", "gy"), P(None, "gx", "gy"))
    return jax.shard_map(body, mesh=mesh, in_specs=in_specs, out_specs=out_specs, check_vma=False)
```

```python
import functools
import math

import jax
import jax.numpy as jnp
import numpy as np
from jax import lax
from jax.experimental import pallas as pl
from jax.experimental.pallas import tpu as pltpu
from jax.sharding import PartitionSpec as P

RADIUS = 128
LAYERS_ALL = 512
MESH = pl.DeviceIdType.MESH
F32 = jnp.float32
BF16 = jnp.bfloat16

DIRS = ((1, 0), (-1, 0), (0, 1), (0, -1))


def halves(table):
    high = table.astype(BF16)
    return high, (table - high.astype(np.float64)).astype(BF16)


def tables(length):
    half = length // 2
    odd = 2 * np.arange(half)[:, None] + 1
    phase = (odd * (2 * np.arange(length)[None, :] - length + 1)) % (4 * length)
    angle = phase * (2.0 * math.pi / (4 * length))
    basis = np.concatenate([np.cos(angle), np.sin(angle)])
    ends = np.split(basis, (RADIUS, length - RADIUS), axis=1)
    basis = np.concatenate([ends[0], ends[2], ends[1]], axis=1)
    ticks = np.arange(half)[None, :]
    kphase = (odd * ticks) % (2 * length)
    weight = np.where(ticks == 0, 1.0, 2.0) * (ticks <= RADIUS) / half
    cosines = np.cos(kphase * (2.0 * math.pi / (2 * length))) * weight
    return halves(basis), halves(np.ascontiguousarray(basis.T)), halves(cosines)


def dot(left, right):
    return lax.dot_general(left, right, (((1,), (0,)), ((), ())), preferred_element_type=F32)


def dot_t(left, right):
    return lax.dot_general(left, right, (((1,), (1,)), ((), ())), preferred_element_type=F32)


def in_hbm(array):
    return pltpu.with_memory_space_constraint(array, pltpu.HBM)


def split(value):
    high = value.astype(BF16)
    return high, (value - high.astype(F32)).astype(BF16)


def product(left, right, how=dot):
    return how(left[0], right[0]) + (how(left[1], right[0]) + how(left[0], right[1]))


def part(refs, rows, cols):
    return refs[0][rows, cols], refs[1][rows, cols]


def put(refs, rows, cols, value):
    refs[0][rows, cols], refs[1][rows, cols] = split(value)


def forward_kernel(
    counts,
    layer_index, density, observed, stations, bas_h, bas_l, tra_h, tra_l, cos_h, cos_l,
    predicted, residual, blocks, spectra, b_h, b_l, t_h, t_l,
    den, obs, sta, c_h, c_l,
    s_h, s_l, z_h, z_l, total, big, win, wait_x, from_x, from_y, from_c,
    index, index_sem, load_sem, send_sem, recv_sem,
):
    gx, gy = lax.axis_index("gx"), lax.axis_index("gy")
    nx, ny = counts
    layers, tile = den.shape[0], den.shape[1]
    length = tile + 2 * RADIUS
    half = length // 2
    low, high, mid = slice(0, RADIUS), slice(RADIUS, 2 * RADIUS), slice(2 * RADIUS, length)
    edge, every = slice(0, 2 * RADIUS), slice(0, length)
    first, last = slice(2 * RADIUS, 3 * RADIUS), slice(length - RADIUS, length)
    own = slice(0, tile)

    def there(dx, dy):
        if dx:
            return gx < nx - 1 if dx > 0 else gx > 0
        return gy < ny - 1 if dy > 0 else gy > 0

    def target(dx, dy):
        return {"gx": gx + dx, "gy": gy + dy}

    barrier = pltpu.get_barrier_semaphore()
    for dx, dy in DIRS:
        @pl.when(there(dx, dy))
        def _(dx=dx, dy=dy):
            pl.semaphore_signal(barrier, inc=1, device_id=target(dx, dy), device_id_type=MESH)

    pairs = ((cos_h, c_h), (cos_l, c_l), (density, den), (tra_h, t_h), (tra_l, t_l), (bas_h, b_h), (bas_l, b_l), (observed, obs), (stations, sta))
    loads = [pltpu.make_async_copy(src, dst, load_sem.at[i]) for i, (src, dst) in enumerate(pairs)]
    index_load = pltpu.make_async_copy(layer_index, index, index_sem)
    index_load.start()
    for load in loads:
        load.start()

    @pl.when(gx == 0)
    def _():
        win[low, mid] = jnp.zeros((RADIUS, tile), F32)

    @pl.when(gx == nx - 1)
    def _():
        win[high, mid] = jnp.zeros((RADIUS, tile), F32)

    @pl.when(gy == 0)
    def _():
        win[:, low] = jnp.zeros((length, RADIUS), F32)

    @pl.when(gy == ny - 1)
    def _():
        win[:, high] = jnp.zeros((length, RADIUS), F32)

    rows = lax.broadcasted_iota(jnp.int32, (half, half), 0).astype(F32)
    cols = lax.broadcasted_iota(jnp.int32, (half, half), 1).astype(F32)
    flat = rows * rows + cols * cols
    index_load.wait()
    loads[0].wait()
    loads[1].wait()
    cosines = (c_h[...], c_l[...])
    for layer in range(layers):
        depth = RADIUS * (0.375 + index[layer].astype(F32) / LAYERS_ALL)
        square = flat + depth * depth
        inverse = lax.rsqrt(square)
        value = (depth * depth) * (inverse * inverse * inverse)
        left = product(cosines, split(value))
        spectra[layer] = product(split(left), cosines, dot_t)

    for load in loads[2:7]:
        load.wait()
    basis, trans, work, mixed = (b_h, b_l), (t_h, t_l), (s_h, s_l), (z_h, z_l)
    bands = [slice(r * half, (r + 1) * half) for r in range(2)]
    for layer in range(layers):
        put(work, own, every, product(split(den[layer]), part(trans, mid, every)))
        spectrum = spectra[layer]
        for band in bands:
            out = product(part(basis, band, mid), part(work, own, every))
            for at in bands:
                term = spectrum * out[:, at]
                if layer == 0:
                    total[band, at] = term
                elif layer < layers - 1:
                    total[band, at] = total[band, at] + term
                else:
                    put(mixed, band, at, total[band, at] + term)

    def remote(kind, k, src, dst):
        return pltpu.make_async_remote_copy(
            src_ref=src, dst_ref=dst, send_sem=send_sem.at[kind, k], recv_sem=recv_sem.at[kind, k],
            device_id=target(*DIRS[k]), device_id_type=MESH,
        )

    beyond = {1: high, -1: low}
    near = {1: last, -1: first}
    far = {1: low, -1: high}

    def fold_corner(k):
        return remote(0, k, big.at[edge, beyond[DIRS[k][1]]], from_c.at[k - 2])

    def fold_y(k):
        return remote(1, k, big.at[mid, beyond[DIRS[k][1]]], from_y.at[k - 2])

    def fold_x(k):
        return remote(1, k, big.at[beyond[DIRS[k][0]], mid], from_x.at[k])

    def halo_x(k):
        side = DIRS[k][0]
        return remote(2, k, win.at[near[side], mid], win.at[far[side], mid])

    def halo_y(k):
        side = DIRS[k][1]
        return remote(2, k, win.at[mid, near[side]], win.at[mid, far[side]])

    def halo_corner(k):
        side = DIRS[k][1]
        return remote(3, k, win.at[edge, near[side]], win.at[edge, far[side]])

    along_x, along_y = (0, 1), (2, 3)

    def start(make, ks):
        for k in ks:
            @pl.when(there(*DIRS[k]))
            def _(k=k):
                make(k).start()

    def sent(make, ks):
        for k in ks:
            @pl.when(there(*DIRS[k]))
            def _(k=k):
                make(k).wait_send()

    def received(make, ks, then=None):
        for k in ks:
            dx, dy = DIRS[k]
            @pl.when(there(-dx, -dy))
            def _(k=k):
                make(k).wait_recv()
                if then is not None:
                    then(k)

    def mix(cs):
        for band in bands:
            put(work, band, cs, product(part(mixed, band, every), part(basis, every, cs)))

    def back(rs, cs):
        big[rs, cs] = product(part(trans, rs, every), part(work, every, cs))

    mix(edge)
    back(edge, edge)
    sides_x = 2 - (gx == 0).astype(jnp.int32) - (gx == nx - 1).astype(jnp.int32)
    sides_y = 2 - (gy == 0).astype(jnp.int32) - (gy == ny - 1).astype(jnp.int32)
    pl.semaphore_wait(barrier, sides_x + sides_y)
    start(fold_corner, along_y)
    mix(mid)
    back(edge, mid)

    def add_corner(k):
        cs = {1: first, -1: last}[DIRS[k][1]]
        big[edge, cs] = big[edge, cs] + from_c[k - 2]

    received(fold_corner, along_y, add_corner)
    start(fold_x, along_x)
    back(mid, edge)
    start(fold_y, along_y)
    back(mid, mid)
    for load in loads[7:]:
        load.wait()

    def add_y(k):
        cs = {1: first, -1: last}[DIRS[k][1]]
        big[mid, cs] = big[mid, cs] + from_y[k - 2]

    def add_x(k):
        rs = {1: first, -1: last}[DIRS[k][0]]
        big[rs, mid] = big[rs, mid] + from_x[k]

    received(fold_y, along_y, add_y)
    received(fold_x, along_x, add_x)
    total_pred = big[mid, mid]
    misfit = sta[...].astype(F32) * (total_pred - obs[...])
    win[mid, mid] = misfit
    start(halo_x, along_x)
    start(halo_y, along_y)
    predicted[...] = total_pred
    residual[...] = misfit

    received(halo_y, along_y)
    put(work, mid, every, product(split(win[mid, :]), part(trans, every, every)))
    for band in bands:
        total[band, :] = product(part(basis, band, mid), part(work, mid, every))

    received(halo_x, along_x)
    start(halo_corner, along_y)
    wait_x[...] = product(split(win[edge, mid]), part(trans, mid, every))
    received(halo_corner, along_y)
    put(work, edge, every, wait_x[...] + product(split(win[edge, edge]), part(trans, edge, every)))
    for band in bands:
        blocks[band, :] = total[band, :] + product(part(basis, band, edge), part(work, edge, every))
    sent(fold_corner, along_y)
    sent(fold_y, along_y)
    sent(fold_x, along_x)
    sent(halo_x, along_x)
    sent(halo_y, along_y)
    sent(halo_corner, along_y)


def adjoint_kernel(
    predicted, residual, blocks, spectra, b_h, b_l, t_h, t_l,
    predicted_out, residual_out, gradient,
    z_h, z_l, w_h, w_l, grad, out_sem,
):
    layers, tile = spectra.shape[0], residual.shape[0]
    length = tile + 2 * RADIUS
    half = length // 2
    mid, every, own = slice(2 * RADIUS, length), slice(0, length), slice(0, tile)
    bands = [slice(r * half, (r + 1) * half) for r in range(2)]
    basis, trans, mixed, work = (b_h, b_l), (t_h, t_l), (z_h, z_l), (w_h, w_l)
    stores = [
        pltpu.make_async_copy(predicted, predicted_out, out_sem.at[0]),
        pltpu.make_async_copy(residual, residual_out, out_sem.at[1]),
    ]
    for store in stores:
        store.start()
    for layer in range(layers):
        spectrum = spectra[layer]
        for band in bands:
            for at in bands:
                put(mixed, band, at, spectrum * blocks[band, at])
        for band in bands:
            put(work, band, own, product(part(mixed, band, every), part(basis, every, mid)))
        grad[layer] = product(part(trans, mid, every), part(work, every, own))
        store = pltpu.make_async_copy(grad.at[layer], gradient.at[layer], out_sem.at[2 + layer])
        store.start()
        stores.append(store)
    for store in stores:
        store.wait()


def solution(mesh):
    counts = (mesh.shape["gx"], mesh.shape["gy"])

    def body(density, observed, stations, layer_index):
        layers, tile = density.shape[0], density.shape[1]
        length = tile + 2 * RADIUS
        half = length // 2
        (bas_h, bas_l), (tra_h, tra_l), (cos_h, cos_l) = tables(length)
        anywhere = pl.BlockSpec(memory_space=pl.ANY)
        vmem = pl.BlockSpec(memory_space=pltpu.VMEM)
        big = pltpu.VMEM((length, length), F32)
        wide = pltpu.VMEM((length, length), BF16)
        small = pltpu.VMEM((half, half), BF16)
        predicted, residual, blocks, spectra, *kept = pl.pallas_call(
            functools.partial(forward_kernel, counts),
            out_shape=(
                pltpu.VMEM((tile, tile), F32),
                pltpu.VMEM((tile, tile), F32),
                pltpu.VMEM((length, length), F32),
                pltpu.VMEM((layers, half, half), F32),
                wide, wide, wide, wide,
            ),
            in_specs=[anywhere] * 10,
            out_specs=(vmem,) * 8,
            scratch_shapes=[
                pltpu.VMEM(density.shape, F32),
                pltpu.VMEM((tile, tile), F32),
                pltpu.VMEM((tile, tile), jnp.int32),
                small, small,
                wide, wide, wide, wide, big, big, big,
                pltpu.VMEM((2 * RADIUS, length), F32),
                pltpu.VMEM((2, RADIUS, tile), F32),
                pltpu.VMEM((2, tile, RADIUS), F32),
                pltpu.VMEM((2, 2 * RADIUS, RADIUS), F32),
                pltpu.SMEM((layers,), jnp.int32),
                pltpu.SemaphoreType.DMA,
                pltpu.SemaphoreType.DMA((9,)),
                pltpu.SemaphoreType.DMA((4, 4)),
                pltpu.SemaphoreType.DMA((4, 4)),
            ],
            compiler_params=pltpu.CompilerParams(
                collective_id=0, has_side_effects=True, vmem_limit_bytes=32 << 20
            ),
            name="forward",
        )(*map(in_hbm, (layer_index, density, observed, stations, bas_h, bas_l, tra_h, tra_l, cos_h, cos_l)))
        return pl.pallas_call(
            adjoint_kernel,
            out_shape=(
                jax.ShapeDtypeStruct((tile, tile), F32),
                jax.ShapeDtypeStruct((tile, tile), F32),
                jax.ShapeDtypeStruct((layers, tile, tile), F32),
            ),
            in_specs=[vmem] * 8,
            out_specs=(anywhere,) * 3,
            scratch_shapes=[
                wide, wide,
                pltpu.VMEM((length, tile), BF16),
                pltpu.VMEM((length, tile), BF16),
                pltpu.VMEM((layers, tile, tile), F32),
                pltpu.SemaphoreType.DMA((2 + layers,)),
            ],
            compiler_params=pltpu.CompilerParams(vmem_limit_bytes=24 << 20),
            name="adjoint",
        )(predicted, residual, blocks, spectra, *kept)

    in_specs = (P(None, "gx", "gy"), P("gx", "gy"), P("gx", "gy"), P())
    out_specs = (P("gx", "gy"), P("gx", "gy"), P(None, "gx", "gy"))
    return jax.shard_map(body, mesh=mesh, in_specs=in_specs, out_specs=out_specs, check_vma=False)
```

```python
import functools
import math

import jax
import jax.numpy as jnp
import numpy as np
from jax import lax
from jax.experimental import pallas as pl
from jax.experimental.pallas import tpu as pltpu
from jax.sharding import PartitionSpec as P

RADIUS = 128
LAYERS_ALL = 512
MESH = pl.DeviceIdType.MESH
F32 = jnp.float32
BF16 = jnp.bfloat16

CHUNKS = 2


def halves(table):
    high = table.astype(BF16)
    return high, (table - high.astype(np.float64)).astype(BF16)


def tables(length):
    half = length // 2
    odd = 2 * np.arange(half)[:, None] + 1
    phase = (odd * (2 * np.arange(length)[None, :] - length + 1)) % (4 * length)
    angle = phase * (2.0 * math.pi / (4 * length))
    basis = np.concatenate([np.cos(angle), np.sin(angle)])
    ends = np.split(basis, (RADIUS, length - RADIUS), axis=1)
    basis = np.concatenate([ends[0], ends[2], ends[1]], axis=1)
    ticks = np.arange(half)[None, :]
    kphase = (odd * ticks) % (2 * length)
    weight = np.where(ticks == 0, 1.0, 2.0) * (ticks <= RADIUS) / half
    cosines = np.cos(kphase * (2.0 * math.pi / (2 * length))) * weight
    return halves(basis), halves(np.ascontiguousarray(basis.T)), halves(cosines)


def dot(left, right):
    return lax.dot_general(left, right, (((1,), (0,)), ((), ())), preferred_element_type=F32)


def dot_t(left, right):
    return lax.dot_general(left, right, (((1,), (1,)), ((), ())), preferred_element_type=F32)


def in_hbm(array):
    return pltpu.with_memory_space_constraint(array, pltpu.HBM)


def split(value):
    high = value.astype(BF16)
    return high, (value - high.astype(F32)).astype(BF16)


def product(left, right, how=dot):
    return how(left[0], right[0]) + (how(left[1], right[0]) + how(left[0], right[1]))


def part(refs, rows, cols):
    return refs[0][rows, cols], refs[1][rows, cols]


def put(refs, rows, cols, value):
    refs[0][rows, cols], refs[1][rows, cols] = split(value)


def forward_kernel(
    counts,
    layer_index, density, observed, stations, bas_h, bas_l, tra_h, tra_l, cos_h, cos_l,
    predicted, residual, blocks, spectra, b_h, b_l, t_h, t_l,
    den, obs, sta, c_h, c_l,
    s_h, s_l, z_h, z_l, total, big, win, wait_x, from_x, from_y, from_c, from_d,
    index, index_sem, load_sem, send_sem, recv_sem,
):
    gx, gy = lax.axis_index("gx"), lax.axis_index("gy")
    nx, ny = counts
    layers, tile = den.shape[0], den.shape[1]
    length = tile + 2 * RADIUS
    half = length // 2
    low, high, mid = slice(0, RADIUS), slice(RADIUS, 2 * RADIUS), slice(2 * RADIUS, length)
    edge, every = slice(0, 2 * RADIUS), slice(0, length)
    first, last = slice(2 * RADIUS, 3 * RADIUS), slice(length - RADIUS, length)
    own = slice(0, tile)

    even = lax.rem(gy, 2) == 0
    partner = gy + jnp.where(even, 1, -1)
    outer = gy + jnp.where(even, -1, 1)
    has_outer = (outer >= 0) & (outer < ny)
    steps = (1, -1)

    def columns(for_even, for_odd):
        return pl.ds(pl.multiple_of(jnp.where(even, for_even, for_odd), RADIUS), RADIUS)

    core_edge, far_edge = columns(RADIUS, 0), columns(0, RADIUS)
    core_near, far_near = columns(length - RADIUS, 2 * RADIUS), columns(2 * RADIUS, length - RADIUS)

    def there(dx):
        return gx < nx - 1 if dx > 0 else gx > 0

    def only_if(condition, act):
        pl.when(condition)(act)

    barrier = pltpu.get_barrier_semaphore()

    def greet(x, y):
        pl.semaphore_signal(barrier, inc=1, device_id={"gx": x, "gy": y}, device_id_type=MESH)

    greet(gx, partner)
    only_if(has_outer, lambda: greet(gx, outer))
    for dx in steps:
        only_if(there(dx), lambda: greet(gx + dx, gy))
        only_if(there(dx) & has_outer, lambda: greet(gx + dx, outer))

    pairs = ((cos_h, c_h), (cos_l, c_l), (density, den), (tra_h, t_h), (tra_l, t_l), (bas_h, b_h), (bas_l, b_l), (observed, obs), (stations, sta))
    loads = [pltpu.make_async_copy(src, dst, load_sem.at[i]) for i, (src, dst) in enumerate(pairs)]
    index_load = pltpu.make_async_copy(layer_index, index, index_sem)
    index_load.start()
    for load in loads:
        load.start()

    @pl.when(gx == 0)
    def _():
        win[low, :] = jnp.zeros((RADIUS, length), F32)

    @pl.when(gx == nx - 1)
    def _():
        win[high, :] = jnp.zeros((RADIUS, length), F32)

    @pl.when(gy == 0)
    def _():
        win[:, low] = jnp.zeros((length, RADIUS), F32)

    @pl.when(gy == ny - 1)
    def _():
        win[:, high] = jnp.zeros((length, RADIUS), F32)

    rows = lax.broadcasted_iota(jnp.int32, (half, half), 0).astype(F32)
    cols = lax.broadcasted_iota(jnp.int32, (half, half), 1).astype(F32)
    flat = rows * rows + cols * cols
    index_load.wait()
    loads[0].wait()
    loads[1].wait()
    cosines = (c_h[...], c_l[...])
    for layer in range(layers):
        depth = RADIUS * (0.375 + index[layer].astype(F32) / LAYERS_ALL)
        square = flat + depth * depth
        inverse = lax.rsqrt(square)
        value = (depth * depth) * (inverse * inverse * inverse)
        left = product(cosines, split(value))
        spectra[layer] = product(split(left), cosines, dot_t)

    for load in loads[2:7]:
        load.wait()
    basis, trans, work, mixed = (b_h, b_l), (t_h, t_l), (s_h, s_l), (z_h, z_l)
    bands = [slice(r * half, (r + 1) * half) for r in range(2)]
    for layer in range(layers):
        put(work, own, every, product(split(den[layer]), part(trans, mid, every)))
        spectrum = spectra[layer]
        for band in bands:
            out = product(part(basis, band, mid), part(work, own, every))
            for at in bands:
                term = spectrum * out[:, at]
                if layer == 0:
                    total[band, at] = term
                elif layer < layers - 1:
                    total[band, at] = total[band, at] + term
                else:
                    put(mixed, band, at, total[band, at] + term)

    def remote(number, src, dst, x, y):
        return pltpu.make_async_remote_copy(
            src_ref=src, dst_ref=dst, send_sem=send_sem.at[number], recv_sem=recv_sem.at[number],
            device_id={"gx": x, "gy": y}, device_id_type=MESH,
        )

    depth_of = RADIUS // CHUNKS

    def piece(rs, c):
        return slice(rs.start + c * depth_of, rs.start + (c + 1) * depth_of)

    beyond = {1: high, -1: low}
    near = {1: last, -1: first}
    far = {1: low, -1: high}
    lands = {1: first, -1: last}
    each = [(c, dx) for c in range(CHUNKS) for dx in steps]

    def numbered(kind, c, dx):
        return 5 + (kind * CHUNKS + c) * 2 + (dx < 0)

    def fold_core():
        return remote(0, big.at[edge, core_edge], from_c, gx, partner)

    def fold_partner():
        return remote(1, big.at[mid, core_edge], from_y.at[0], gx, partner)

    def fold_outer():
        return remote(2, big.at[mid, far_edge], from_y.at[1], gx, outer)

    def fold_x(c, dx):
        rs = slice(c * depth_of, (c + 1) * depth_of)
        return remote(numbered(0, c, dx), big.at[piece(beyond[dx], c), mid], from_x.at[int(dx < 0), rs], gx + dx, gy)

    def fold_d(c, dx):
        rs = slice(c * depth_of, (c + 1) * depth_of)
        return remote(numbered(1, c, dx), big.at[piece(beyond[dx], c), far_edge], from_d.at[int(dx < 0), rs], gx + dx, outer)

    def halo_partner():
        return remote(3, win.at[mid, core_near], win.at[mid, far_edge], gx, partner)

    def halo_outer():
        return remote(4, win.at[mid, far_near], win.at[mid, core_edge], gx, outer)

    def halo_x(c, dx):
        return remote(numbered(2, c, dx), win.at[piece(near[dx], c), mid], win.at[piece(far[dx], c), mid], gx + dx, gy)

    def halo_d(c, dx):
        return remote(numbered(3, c, dx), win.at[piece(near[dx], c), far_near], win.at[piece(far[dx], c), core_edge], gx + dx, outer)

    def halo_core(c, dx):
        return remote(numbered(4, c, dx), win.at[piece(far[dx], c), core_near], win.at[piece(far[dx], c), far_edge], gx, partner)

    def mix(cs):
        for band in bands:
            put(work, band, cs, product(part(mixed, band, every), part(basis, every, cs)))

    def back(rs, cs):
        big[rs, cs] = product(part(trans, rs, every), part(work, every, cs))

    mix(edge)
    back(edge, edge)
    sides = 2 - (gx == 0).astype(jnp.int32) - (gx == nx - 1).astype(jnp.int32)
    pl.semaphore_wait(barrier, (sides + 1) * jnp.where(has_outer, 2, 1))
    fold_core().start()
    for c, dx in each:
        only_if(there(dx) & has_outer, lambda: fold_d(c, dx).start())
    mix(mid)
    back(edge, mid)
    fold_core().wait_recv()
    big[edge, core_near] = big[edge, core_near] + from_c[...]
    for c, dx in each:
        only_if(there(dx), lambda: fold_x(c, dx).start())
    back(mid, edge)
    fold_partner().start()
    only_if(has_outer, lambda: fold_outer().start())
    back(mid, mid)
    for load in loads[7:]:
        load.wait()

    fold_partner().wait_recv()
    big[mid, core_near] = big[mid, core_near] + from_y[0]

    @pl.when(has_outer)
    def _():
        fold_outer().wait_recv()
        big[mid, far_near] = big[mid, far_near] + from_y[1]

    for c, dx in each:
        rs = piece(lands[dx], c)
        tile_rows = slice(rs.start - 2 * RADIUS, rs.stop - 2 * RADIUS)
        at = slice(c * depth_of, (c + 1) * depth_of)

        @pl.when(there(-dx))
        def _():
            fold_x(c, dx).wait_recv()
            big[rs, mid] = big[rs, mid] + from_x[int(dx < 0), at]

        @pl.when(there(-dx) & has_outer)
        def _():
            fold_d(c, dx).wait_recv()
            big[rs, far_near] = big[rs, far_near] + from_d[int(dx < 0), at]

        ahead = big[rs, mid]
        win[rs, mid] = sta[tile_rows, :].astype(F32) * (ahead - obs[tile_rows, :])
        only_if(there(-dx), lambda: halo_x(c, -dx).start())
        only_if(there(-dx) & has_outer, lambda: halo_d(c, -dx).start())

    halo_partner().start()
    only_if(has_outer, lambda: halo_outer().start())
    predicted[...] = big[mid, mid]
    residual[...] = win[mid, mid]

    halo_partner().wait_recv()
    only_if(has_outer, lambda: halo_outer().wait_recv())
    put(work, mid, every, product(split(win[mid, :]), part(trans, every, every)))
    for band in bands:
        total[band, :] = product(part(basis, band, mid), part(work, mid, every))

    for c, dx in each:
        @pl.when(there(-dx))
        def _():
            halo_x(c, dx).wait_recv()
            halo_core(c, dx).start()

    wait_x[...] = product(split(win[edge, mid]), part(trans, mid, every))
    for c, dx in each:
        only_if(there(-dx), lambda: halo_core(c, dx).wait_recv())
        only_if(there(-dx) & has_outer, lambda: halo_d(c, dx).wait_recv())
    put(work, edge, every, wait_x[...] + product(split(win[edge, edge]), part(trans, edge, every)))
    for band in bands:
        blocks[band, :] = total[band, :] + product(part(basis, band, edge), part(work, edge, every))

    fold_core().wait_send()
    fold_partner().wait_send()
    halo_partner().wait_send()

    @pl.when(has_outer)
    def _():
        fold_outer().wait_send()
        halo_outer().wait_send()

    for c, dx in each:
        @pl.when(there(dx))
        def _():
            fold_x(c, dx).wait_send()
            halo_x(c, dx).wait_send()

        @pl.when(there(dx) & has_outer)
        def _():
            fold_d(c, dx).wait_send()
            halo_d(c, dx).wait_send()

        only_if(there(-dx), lambda: halo_core(c, dx).wait_send())


def adjoint_kernel(
    predicted, residual, blocks, spectra, b_h, b_l, t_h, t_l,
    predicted_out, residual_out, gradient,
    z_h, z_l, w_h, w_l, grad, out_sem,
):
    layers, tile = spectra.shape[0], residual.shape[0]
    length = tile + 2 * RADIUS
    half = length // 2
    mid, every, own = slice(2 * RADIUS, length), slice(0, length), slice(0, tile)
    bands = [slice(r * half, (r + 1) * half) for r in range(2)]
    basis, trans, mixed, work = (b_h, b_l), (t_h, t_l), (z_h, z_l), (w_h, w_l)
    stores = [
        pltpu.make_async_copy(predicted, predicted_out, out_sem.at[0]),
        pltpu.make_async_copy(residual, residual_out, out_sem.at[1]),
    ]
    for store in stores:
        store.start()
    for layer in range(layers):
        spectrum = spectra[layer]
        for band in bands:
            for at in bands:
                put(mixed, band, at, spectrum * blocks[band, at])
        for band in bands:
            put(work, band, own, product(part(mixed, band, every), part(basis, every, mid)))
        grad[layer] = product(part(trans, mid, every), part(work, every, own))
        store = pltpu.make_async_copy(grad.at[layer], gradient.at[layer], out_sem.at[2 + layer])
        store.start()
        stores.append(store)
    for store in stores:
        store.wait()


def solution(mesh):
    counts = (mesh.shape["gx"], mesh.shape["gy"])

    def body(density, observed, stations, layer_index):
        layers, tile = density.shape[0], density.shape[1]
        length = tile + 2 * RADIUS
        half = length // 2
        (bas_h, bas_l), (tra_h, tra_l), (cos_h, cos_l) = tables(length)
        anywhere = pl.BlockSpec(memory_space=pl.ANY)
        vmem = pl.BlockSpec(memory_space=pltpu.VMEM)
        big = pltpu.VMEM((length, length), F32)
        wide = pltpu.VMEM((length, length), BF16)
        small = pltpu.VMEM((half, half), BF16)
        predicted, residual, blocks, spectra, *kept = pl.pallas_call(
            functools.partial(forward_kernel, counts),
            out_shape=(
                pltpu.VMEM((tile, tile), F32),
                pltpu.VMEM((tile, tile), F32),
                pltpu.VMEM((length, length), F32),
                pltpu.VMEM((layers, half, half), F32),
                wide, wide, wide, wide,
            ),
            in_specs=[anywhere] * 10,
            out_specs=(vmem,) * 8,
            scratch_shapes=[
                pltpu.VMEM(density.shape, F32),
                pltpu.VMEM((tile, tile), F32),
                pltpu.VMEM((tile, tile), jnp.int32),
                small, small,
                wide, wide, wide, wide, big, big, big,
                pltpu.VMEM((2 * RADIUS, length), F32),
                pltpu.VMEM((2, RADIUS, tile), F32),
                pltpu.VMEM((2, tile, RADIUS), F32),
                pltpu.VMEM((2 * RADIUS, RADIUS), F32),
                pltpu.VMEM((2, RADIUS, RADIUS), F32),
                pltpu.SMEM((layers,), jnp.int32),
                pltpu.SemaphoreType.DMA,
                pltpu.SemaphoreType.DMA((9,)),
                pltpu.SemaphoreType.DMA((5 + 10 * CHUNKS,)),
                pltpu.SemaphoreType.DMA((5 + 10 * CHUNKS,)),
            ],
            compiler_params=pltpu.CompilerParams(
                collective_id=0, has_side_effects=True, vmem_limit_bytes=32 << 20
            ),
            name="forward",
        )(*map(in_hbm, (layer_index, density, observed, stations, bas_h, bas_l, tra_h, tra_l, cos_h, cos_l)))
        return pl.pallas_call(
            adjoint_kernel,
            out_shape=(
                jax.ShapeDtypeStruct((tile, tile), F32),
                jax.ShapeDtypeStruct((tile, tile), F32),
                jax.ShapeDtypeStruct((layers, tile, tile), F32),
            ),
            in_specs=[vmem] * 8,
            out_specs=(anywhere,) * 3,
            scratch_shapes=[
                wide, wide,
                pltpu.VMEM((length, tile), BF16),
                pltpu.VMEM((length, tile), BF16),
                pltpu.VMEM((layers, tile, tile), F32),
                pltpu.SemaphoreType.DMA((2 + layers,)),
            ],
            compiler_params=pltpu.CompilerParams(vmem_limit_bytes=24 << 20),
            name="adjoint",
        )(predicted, residual, blocks, spectra, *kept)

    in_specs = (P(None, "gx", "gy"), P("gx", "gy"), P("gx", "gy"), P())
    out_specs = (P("gx", "gy"), P("gx", "gy"), P(None, "gx", "gy"))
    return jax.shard_map(body, mesh=mesh, in_specs=in_specs, out_specs=out_specs, check_vma=False)
```

```python
import functools
import math

import jax
import jax.numpy as jnp
import numpy as np
from jax import lax
from jax.experimental import pallas as pl
from jax.experimental.pallas import tpu as pltpu
from jax.sharding import PartitionSpec as P

RADIUS = 128
LAYERS_ALL = 512
MESH = pl.DeviceIdType.MESH
F32 = jnp.float32
BF16 = jnp.bfloat16

CHUNKS = 1


def halves(table):
    high = table.astype(BF16)
    return high, (table - high.astype(np.float64)).astype(BF16)


def tables(length):
    half = length // 2
    odd = 2 * np.arange(half)[:, None] + 1
    phase = (odd * (2 * np.arange(length)[None, :] - length + 1)) % (4 * length)
    angle = phase * (2.0 * math.pi / (4 * length))
    basis = np.concatenate([np.cos(angle), np.sin(angle)])
    ends = np.split(basis, (RADIUS, length - RADIUS), axis=1)
    basis = np.concatenate([ends[0], ends[2], ends[1]], axis=1)
    ticks = np.arange(half)[None, :]
    kphase = (odd * ticks) % (2 * length)
    weight = np.where(ticks == 0, 1.0, 2.0) * (ticks <= RADIUS) / half
    cosines = np.cos(kphase * (2.0 * math.pi / (2 * length))) * weight
    return halves(basis), halves(np.ascontiguousarray(basis.T)), halves(cosines)


def dot(left, right):
    return lax.dot_general(left, right, (((1,), (0,)), ((), ())), preferred_element_type=F32)


def dot_t(left, right):
    return lax.dot_general(left, right, (((1,), (1,)), ((), ())), preferred_element_type=F32)


def in_hbm(array):
    return pltpu.with_memory_space_constraint(array, pltpu.HBM)


def split(value):
    high = value.astype(BF16)
    return high, (value - high.astype(F32)).astype(BF16)


def product(left, right, how=dot):
    return how(left[0], right[0]) + (how(left[1], right[0]) + how(left[0], right[1]))


def part(refs, rows, cols):
    return refs[0][rows, cols], refs[1][rows, cols]


def put(refs, rows, cols, value):
    refs[0][rows, cols], refs[1][rows, cols] = split(value)


def forward_kernel(
    counts,
    layer_index, density, observed, stations, bas_h, bas_l, tra_h, tra_l, cos_h, cos_l,
    predicted, residual, blocks, spectra, b_h, b_l, t_h, t_l,
    den, obs, sta, c_h, c_l,
    s_h, s_l, z_h, z_l, total, big, win, wait_x, from_x, from_y, from_c, from_d,
    index, index_sem, load_sem, send_sem, recv_sem,
):
    gx, gy = lax.axis_index("gx"), lax.axis_index("gy")
    nx, ny = counts
    layers, tile = den.shape[0], den.shape[1]
    length = tile + 2 * RADIUS
    half = length // 2
    low, high, mid = slice(0, RADIUS), slice(RADIUS, 2 * RADIUS), slice(2 * RADIUS, length)
    edge, every = slice(0, 2 * RADIUS), slice(0, length)
    first, last = slice(2 * RADIUS, 3 * RADIUS), slice(length - RADIUS, length)

    even = lax.rem(gy, 2) == 0
    partner = gy + jnp.where(even, 1, -1)
    outer = gy + jnp.where(even, -1, 1)
    has_outer = (outer >= 0) & (outer < ny)
    steps = (1, -1)

    def columns(for_even, for_odd):
        return pl.ds(pl.multiple_of(jnp.where(even, for_even, for_odd), RADIUS), RADIUS)

    core_edge, far_edge = columns(RADIUS, 0), columns(0, RADIUS)
    core_near, far_near = columns(length - RADIUS, 2 * RADIUS), columns(2 * RADIUS, length - RADIUS)

    def there(dx):
        return gx < nx - 1 if dx > 0 else gx > 0

    def only_if(condition, act):
        pl.when(condition)(act)

    barrier = pltpu.get_barrier_semaphore()

    def greet(x, y):
        pl.semaphore_signal(barrier, inc=1, device_id={"gx": x, "gy": y}, device_id_type=MESH)

    greet(gx, partner)
    only_if(has_outer, lambda: greet(gx, outer))
    for dx in steps:
        only_if(there(dx), lambda: greet(gx + dx, gy))
        only_if(there(dx) & has_outer, lambda: greet(gx + dx, outer))

    pairs = [(cos_h, c_h), (cos_l, c_l)]
    pairs += [(density.at[layer], den.at[layer]) for layer in range(layers)]
    pairs += [(tra_h.at[mid], t_h.at[mid]), (tra_l.at[mid], t_l.at[mid])]
    pairs += [(bas_h.at[:, mid], b_h.at[:, mid]), (bas_l.at[:, mid], b_l.at[:, mid])]
    pairs += [(bas_h.at[:, edge], b_h.at[:, edge]), (bas_l.at[:, edge], b_l.at[:, edge])]
    pairs += [(tra_h.at[edge], t_h.at[edge]), (tra_l.at[edge], t_l.at[edge]), (observed, obs), (stations, sta)]
    loads = [pltpu.make_async_copy(src, dst, load_sem.at[i]) for i, (src, dst) in enumerate(pairs)]
    index_load = pltpu.make_async_copy(layer_index, index, index_sem)
    index_load.start()
    for load in loads[: layers + 6]:
        load.start()

    @pl.when(gx == 0)
    def _():
        win[low, :] = jnp.zeros((RADIUS, length), F32)

    @pl.when(gx == nx - 1)
    def _():
        win[high, :] = jnp.zeros((RADIUS, length), F32)

    @pl.when(gy == 0)
    def _():
        win[:, low] = jnp.zeros((length, RADIUS), F32)

    @pl.when(gy == ny - 1)
    def _():
        win[:, high] = jnp.zeros((length, RADIUS), F32)

    rows = lax.broadcasted_iota(jnp.int32, (half, half), 0).astype(F32)
    cols = lax.broadcasted_iota(jnp.int32, (half, half), 1).astype(F32)
    flat = rows * rows + cols * cols
    index_load.wait()
    loads[0].wait()
    loads[1].wait()
    cosines = (c_h[...], c_l[...])
    for layer in range(layers):
        depth = RADIUS * (0.375 + index[layer].astype(F32) / LAYERS_ALL)
        square = flat + depth * depth
        inverse = lax.rsqrt(square)
        value = (depth * depth) * (inverse * inverse * inverse)
        left = product(cosines, split(value))
        spectra[layer] = product(split(left), cosines, dot_t)

    for load in loads[2 : layers + 6]:
        load.wait()
    for load in loads[layers + 6 :]:
        load.start()
    basis, trans, work, mixed = (b_h, b_l), (t_h, t_l), (s_h, s_l), (z_h, z_l)
    bands = [slice(r * half, (r + 1) * half) for r in range(2)]
    for layer in range(layers):
        own = slice(layer % 2 * tile, (layer % 2 + 1) * tile)
        put(work, own, every, product(split(den[layer]), part(trans, mid, every)))
        spectrum = spectra[layer]
        for band in bands:
            out = product(part(basis, band, mid), part(work, own, every))
            for at in bands:
                term = spectrum * out[:, at]
                if layer == 0:
                    total[band, at] = term
                elif layer < layers - 1:
                    total[band, at] = total[band, at] + term
                else:
                    put(mixed, band, at, total[band, at] + term)

    def remote(number, src, dst, x, y):
        return pltpu.make_async_remote_copy(
            src_ref=src, dst_ref=dst, send_sem=send_sem.at[number], recv_sem=recv_sem.at[number],
            device_id={"gx": x, "gy": y}, device_id_type=MESH,
        )

    depth_of = RADIUS // CHUNKS

    def piece(rs, c):
        return slice(rs.start + c * depth_of, rs.start + (c + 1) * depth_of)

    beyond = {1: high, -1: low}
    near = {1: last, -1: first}
    far = {1: low, -1: high}
    lands = {1: first, -1: last}
    each = [(c, dx) for c in range(CHUNKS) for dx in steps]

    def numbered(kind, c, dx):
        return 3 + (kind * CHUNKS + c) * 2 + (dx < 0)

    def fold_core():
        return remote(0, big.at[edge, core_edge], from_c, gx, partner)

    def fold_partner():
        return remote(1, big.at[mid, core_edge], from_y.at[0], gx, partner)

    def fold_outer():
        return remote(2, big.at[mid, far_edge], from_y.at[1], gx, outer)

    def fold_x(c, dx):
        rs = slice(c * depth_of, (c + 1) * depth_of)
        return remote(numbered(0, c, dx), big.at[piece(beyond[dx], c), mid], from_x.at[int(dx < 0), rs], gx + dx, gy)

    def fold_d(c, dx):
        rs = slice(c * depth_of, (c + 1) * depth_of)
        return remote(numbered(1, c, dx), big.at[piece(beyond[dx], c), far_edge], from_d.at[int(dx < 0), rs], gx + dx, outer)

    def halo_partner(c, dx):
        rs = piece(lands[dx], c)
        return remote(numbered(5, c, dx), win.at[rs, core_near], win.at[rs, far_edge], gx, partner)

    def halo_outer(c, dx):
        rs = piece(lands[dx], c)
        return remote(numbered(6, c, dx), win.at[rs, far_near], win.at[rs, core_edge], gx, outer)

    def halo_x(c, dx):
        return remote(numbered(2, c, dx), win.at[piece(near[dx], c), mid], win.at[piece(far[dx], c), mid], gx + dx, gy)

    def halo_d(c, dx):
        return remote(numbered(3, c, dx), win.at[piece(near[dx], c), far_near], win.at[piece(far[dx], c), core_edge], gx + dx, outer)

    def halo_core(c, dx):
        return remote(numbered(4, c, dx), win.at[piece(far[dx], c), core_near], win.at[piece(far[dx], c), far_edge], gx, partner)

    def mix(cs):
        for band in bands:
            put(work, band, cs, product(part(mixed, band, every), part(basis, every, cs)))

    def back(rs, cs):
        big[rs, cs] = product(part(trans, rs, every), part(work, every, cs))

    for load in loads[layers + 6 : layers + 10]:
        load.wait()
    mix(edge)
    back(edge, edge)
    sides = 2 - (gx == 0).astype(jnp.int32) - (gx == nx - 1).astype(jnp.int32)
    pl.semaphore_wait(barrier, (sides + 1) * jnp.where(has_outer, 2, 1))
    fold_core().start()
    for dx in steps:
        only_if(there(dx) & has_outer, lambda: fold_d(0, dx).start())
    mix(mid)
    back(edge, mid)
    fold_core().wait_recv()
    big[edge, core_near] = big[edge, core_near] + from_c[...]
    for dx in steps:
        only_if(there(dx), lambda: fold_x(0, dx).start())
    back(mid, edge)
    fold_partner().start()
    only_if(has_outer, lambda: fold_outer().start())
    for c in range(1, CHUNKS):
        for dx in steps:
            @pl.when(there(dx))
            def _():
                fold_x(c, dx).start()

            only_if(there(dx) & has_outer, lambda: fold_d(c, dx).start())
    back(mid, mid)
    for load in loads[layers + 10 :]:
        load.wait()

    fold_partner().wait_recv()
    big[mid, core_near] = big[mid, core_near] + from_y[0]

    @pl.when(has_outer)
    def _():
        fold_outer().wait_recv()
        big[mid, far_near] = big[mid, far_near] + from_y[1]

    for c, dx in each:
        rs = piece(lands[dx], c)
        tile_rows = slice(rs.start - 2 * RADIUS, rs.stop - 2 * RADIUS)
        at = slice(c * depth_of, (c + 1) * depth_of)

        @pl.when(there(-dx))
        def _():
            fold_x(c, dx).wait_recv()
            big[rs, mid] = big[rs, mid] + from_x[int(dx < 0), at]

        @pl.when(there(-dx) & has_outer)
        def _():
            fold_d(c, dx).wait_recv()
            big[rs, far_near] = big[rs, far_near] + from_d[int(dx < 0), at]

        ahead = big[rs, mid]
        win[rs, mid] = sta[tile_rows, :].astype(F32) * (ahead - obs[tile_rows, :])
        only_if(there(-dx), lambda: halo_x(c, -dx).start())
        only_if(there(-dx) & has_outer, lambda: halo_d(c, -dx).start())
        halo_partner(c, dx).start()
        only_if(has_outer, lambda: halo_outer(c, dx).start())

    predicted[...] = big[mid, mid]
    residual[...] = win[mid, mid]

    for c, dx in each:
        halo_partner(c, dx).wait_recv()
        only_if(has_outer, lambda: halo_outer(c, dx).wait_recv())
    put(work, mid, every, product(split(win[mid, :]), part(trans, every, every)))
    for band in bands:
        total[band, :] = product(part(basis, band, mid), part(work, mid, every))

    for c, dx in each:
        @pl.when(there(-dx))
        def _():
            halo_x(c, dx).wait_recv()
            halo_core(c, dx).start()

    wait_x[...] = product(split(win[edge, mid]), part(trans, mid, every))
    for c, dx in each:
        only_if(there(-dx), lambda: halo_core(c, dx).wait_recv())
        only_if(there(-dx) & has_outer, lambda: halo_d(c, dx).wait_recv())
    put(work, edge, every, wait_x[...] + product(split(win[edge, edge]), part(trans, edge, every)))
    for band in bands:
        blocks[band, :] = total[band, :] + product(part(basis, band, edge), part(work, edge, every))

    fold_core().wait_send()
    fold_partner().wait_send()
    only_if(has_outer, lambda: fold_outer().wait_send())
    for c, dx in each:
        halo_partner(c, dx).wait_send()
        only_if(has_outer, lambda: halo_outer(c, dx).wait_send())

        @pl.when(there(dx))
        def _():
            fold_x(c, dx).wait_send()
            halo_x(c, dx).wait_send()

        @pl.when(there(dx) & has_outer)
        def _():
            fold_d(c, dx).wait_send()
            halo_d(c, dx).wait_send()

        only_if(there(-dx), lambda: halo_core(c, dx).wait_send())


def adjoint_kernel(
    predicted, residual, blocks, spectra, b_h, b_l, t_h, t_l,
    predicted_out, residual_out, gradient,
    z_h, z_l, w_h, w_l, grad, out_sem,
):
    layers, tile = spectra.shape[0], residual.shape[0]
    length = tile + 2 * RADIUS
    half = length // 2
    mid, every, own = slice(2 * RADIUS, length), slice(0, length), slice(0, tile)
    bands = [slice(r * half, (r + 1) * half) for r in range(2)]
    basis, trans = (b_h, b_l), (t_h, t_l)
    stores = [
        pltpu.make_async_copy(predicted, predicted_out, out_sem.at[0]),
        pltpu.make_async_copy(residual, residual_out, out_sem.at[1]),
    ]
    for store in stores:
        store.start()
    for layer in range(layers):
        spectrum = spectra[layer]
        mixed, work = (z_h.at[layer], z_l.at[layer]), (w_h.at[layer], w_l.at[layer])
        for band in bands:
            for at in bands:
                put(mixed, band, at, spectrum * blocks[band, at])
            put(work, band, own, product(part(mixed, band, every), part(basis, every, mid)))
    for layer in range(layers):
        work = (w_h.at[layer], w_l.at[layer])
        for n in range(2):
            rs = slice(n * RADIUS, (n + 1) * RADIUS)
            inner = slice(mid.start + n * RADIUS, mid.start + (n + 1) * RADIUS)
            grad[layer, rs] = product(part(trans, inner, every), part(work, every, own))
            store = pltpu.make_async_copy(grad.at[layer, rs], gradient.at[layer, rs], out_sem.at[2 + 2 * layer + n])
            store.start()
            stores.append(store)
    for store in stores:
        store.wait()


def solution(mesh):
    counts = (mesh.shape["gx"], mesh.shape["gy"])

    def body(density, observed, stations, layer_index):
        layers, tile = density.shape[0], density.shape[1]
        length = tile + 2 * RADIUS
        half = length // 2
        (bas_h, bas_l), (tra_h, tra_l), (cos_h, cos_l) = tables(length)
        anywhere = pl.BlockSpec(memory_space=pl.ANY)
        vmem = pl.BlockSpec(memory_space=pltpu.VMEM)
        big = pltpu.VMEM((length, length), F32)
        wide = pltpu.VMEM((length, length), BF16)
        small = pltpu.VMEM((half, half), BF16)
        predicted, residual, blocks, spectra, *kept = pl.pallas_call(
            functools.partial(forward_kernel, counts),
            out_shape=(
                pltpu.VMEM((tile, tile), F32),
                pltpu.VMEM((tile, tile), F32),
                pltpu.VMEM((length, length), F32),
                pltpu.VMEM((layers, half, half), F32),
                wide, wide, wide, wide,
            ),
            in_specs=[anywhere] * 10,
            out_specs=(vmem,) * 8,
            scratch_shapes=[
                pltpu.VMEM(density.shape, F32),
                pltpu.VMEM((tile, tile), F32),
                pltpu.VMEM((tile, tile), jnp.int32),
                small, small,
                wide, wide, wide, wide, big, big, big,
                pltpu.VMEM((2 * RADIUS, length), F32),
                pltpu.VMEM((2, RADIUS, tile), F32),
                pltpu.VMEM((2, tile, RADIUS), F32),
                pltpu.VMEM((2 * RADIUS, RADIUS), F32),
                pltpu.VMEM((2, RADIUS, RADIUS), F32),
                pltpu.SMEM((layers,), jnp.int32),
                pltpu.SemaphoreType.DMA,
                pltpu.SemaphoreType.DMA((layers + 12,)),
                pltpu.SemaphoreType.DMA((3 + 14 * CHUNKS,)),
                pltpu.SemaphoreType.DMA((3 + 14 * CHUNKS,)),
            ],
            compiler_params=pltpu.CompilerParams(
                collective_id=0, has_side_effects=True, vmem_limit_bytes=32 << 20
            ),
            name="forward",
        )(*map(in_hbm, (layer_index, density, observed, stations, bas_h, bas_l, tra_h, tra_l, cos_h, cos_l)))
        return pl.pallas_call(
            adjoint_kernel,
            out_shape=(
                jax.ShapeDtypeStruct((tile, tile), F32),
                jax.ShapeDtypeStruct((tile, tile), F32),
                jax.ShapeDtypeStruct((layers, tile, tile), F32),
            ),
            in_specs=[vmem] * 8,
            out_specs=(anywhere,) * 3,
            scratch_shapes=[
                pltpu.VMEM((layers, length, length), BF16),
                pltpu.VMEM((layers, length, length), BF16),
                pltpu.VMEM((layers, length, tile), BF16),
                pltpu.VMEM((layers, length, tile), BF16),
                pltpu.VMEM((layers, tile, tile), F32),
                pltpu.SemaphoreType.DMA((2 + 2 * layers,)),
            ],
            compiler_params=pltpu.CompilerParams(vmem_limit_bytes=24 << 20),
            name="adjoint",
        )(predicted, residual, blocks, spectra, *kept)

    in_specs = (P(None, "gx", "gy"), P("gx", "gy"), P("gx", "gy"), P())
    out_specs = (P("gx", "gy"), P("gx", "gy"), P(None, "gx", "gy"))
    return jax.shard_map(body, mesh=mesh, in_specs=in_specs, out_specs=out_specs, check_vma=False)
```

```python
import functools
import math

import jax
import jax.numpy as jnp
import numpy as np
from jax import lax
from jax.experimental import pallas as pl
from jax.experimental.pallas import tpu as pltpu
from jax.sharding import PartitionSpec as P

RADIUS = 128
LAYERS_ALL = 512
MESH = pl.DeviceIdType.MESH
F32 = jnp.float32
BF16 = jnp.bfloat16

CHUNKS = 1


def halves(table):
    high = table.astype(BF16)
    return high, (table - high.astype(np.float64)).astype(BF16)


def tables(length):
    half = length // 2
    odd = 2 * np.arange(half)[:, None] + 1
    phase = (odd * (2 * np.arange(length)[None, :] - length + 1)) % (4 * length)
    angle = phase * (2.0 * math.pi / (4 * length))
    basis = np.concatenate([np.cos(angle), np.sin(angle)])
    ends = np.split(basis, (RADIUS, length - RADIUS), axis=1)
    basis = np.concatenate([ends[0], ends[2], ends[1]], axis=1)
    ticks = np.arange(half)[None, :]
    kphase = (odd * ticks) % (2 * length)
    weight = np.where(ticks == 0, 1.0, 2.0) * (ticks <= RADIUS) / half
    cosines = np.cos(kphase * (2.0 * math.pi / (2 * length))) * weight
    return halves(basis), halves(np.ascontiguousarray(basis.T)), halves(cosines)


def dot(left, right):
    return lax.dot_general(left, right, (((1,), (0,)), ((), ())), preferred_element_type=F32)


def dot_t(left, right):
    return lax.dot_general(left, right, (((1,), (1,)), ((), ())), preferred_element_type=F32)


def in_hbm(array):
    return pltpu.with_memory_space_constraint(array, pltpu.HBM)


def split(value):
    high = value.astype(BF16)
    return high, (value - high.astype(F32)).astype(BF16)


def product(left, right, how=dot):
    return how(left[0], right[0]) + (how(left[1], right[0]) + how(left[0], right[1]))


def part(refs, rows, cols):
    return refs[0][rows, cols], refs[1][rows, cols]


def put(refs, rows, cols, value):
    refs[0][rows, cols], refs[1][rows, cols] = split(value)


def forward_kernel(
    counts,
    layer_index, density, observed, stations, bas_h, bas_l, tra_h, tra_l, cos_h, cos_l,
    predicted, residual, blocks, spectra, b_h, b_l, t_h, t_l,
    den, obs, sta, c_h, c_l,
    s_h, s_l, z_h, z_l, total, big, win, wait_x, from_x, from_y, from_c, from_d,
    index, index_sem, load_sem, send_sem, recv_sem,
):
    gx, gy = lax.axis_index("gx"), lax.axis_index("gy")
    nx, ny = counts
    layers, tile = den.shape[0], den.shape[1]
    length = tile + 2 * RADIUS
    half = length // 2
    low, high, mid = slice(0, RADIUS), slice(RADIUS, 2 * RADIUS), slice(2 * RADIUS, length)
    edge, every = slice(0, 2 * RADIUS), slice(0, length)
    first, last = slice(2 * RADIUS, 3 * RADIUS), slice(length - RADIUS, length)

    even = lax.rem(gy, 2) == 0
    partner = gy + jnp.where(even, 1, -1)
    outer = gy + jnp.where(even, -1, 1)
    has_outer = (outer >= 0) & (outer < ny)
    steps = (1, -1)

    def columns(for_even, for_odd):
        return pl.ds(pl.multiple_of(jnp.where(even, for_even, for_odd), RADIUS), RADIUS)

    core_edge, far_edge = columns(RADIUS, 0), columns(0, RADIUS)
    core_near, far_near = columns(length - RADIUS, 2 * RADIUS), columns(2 * RADIUS, length - RADIUS)

    def there(dx):
        return gx < nx - 1 if dx > 0 else gx > 0

    def only_if(condition, act):
        pl.when(condition)(act)

    barrier = pltpu.get_barrier_semaphore()

    def greet(x, y):
        pl.semaphore_signal(barrier, inc=1, device_id={"gx": x, "gy": y}, device_id_type=MESH)

    only_if(has_outer, lambda: greet(gx, outer))
    greet(gx, partner)
    for dx in steps:
        only_if(there(dx), lambda: greet(gx + dx, gy))
    for dx in steps:
        only_if(there(dx) & has_outer, lambda: greet(gx + dx, outer))

    pairs = [(cos_h, c_h), (cos_l, c_l)]
    pairs += [(density.at[layer], den.at[layer]) for layer in range(layers)]
    pairs += [(tra_h.at[mid], t_h.at[mid]), (tra_l.at[mid], t_l.at[mid])]
    pairs += [(bas_h.at[:, mid], b_h.at[:, mid]), (bas_l.at[:, mid], b_l.at[:, mid])]
    pairs += [(bas_h.at[:, edge], b_h.at[:, edge]), (bas_l.at[:, edge], b_l.at[:, edge])]
    pairs += [(tra_h.at[edge], t_h.at[edge]), (tra_l.at[edge], t_l.at[edge]), (observed, obs), (stations, sta)]
    loads = [pltpu.make_async_copy(src, dst, load_sem.at[i]) for i, (src, dst) in enumerate(pairs)]
    index_load = pltpu.make_async_copy(layer_index, index, index_sem)
    index_load.start()
    for load in loads[: layers + 6]:
        load.start()

    @pl.when(gx == 0)
    def _():
        win[low, :] = jnp.zeros((RADIUS, length), F32)

    @pl.when(gx == nx - 1)
    def _():
        win[high, :] = jnp.zeros((RADIUS, length), F32)

    @pl.when(gy == 0)
    def _():
        win[:, low] = jnp.zeros((length, RADIUS), F32)

    @pl.when(gy == ny - 1)
    def _():
        win[:, high] = jnp.zeros((length, RADIUS), F32)

    rows = lax.broadcasted_iota(jnp.int32, (half, half), 0).astype(F32)
    cols = lax.broadcasted_iota(jnp.int32, (half, half), 1).astype(F32)
    flat = rows * rows + cols * cols
    index_load.wait()
    loads[0].wait()
    loads[1].wait()
    cosines = (c_h[...], c_l[...])
    for layer in range(layers):
        depth = RADIUS * (0.375 + index[layer].astype(F32) / LAYERS_ALL)
        square = flat + depth * depth
        inverse = lax.rsqrt(square)
        value = (depth * depth) * (inverse * inverse * inverse)
        left = product(cosines, split(value))
        spectra[layer] = product(split(left), cosines, dot_t)

    for load in loads[2 : layers + 6]:
        load.wait()
    for load in loads[layers + 6 :]:
        load.start()
    basis, trans, work, mixed = (b_h, b_l), (t_h, t_l), (s_h, s_l), (z_h, z_l)
    bands = [slice(r * half, (r + 1) * half) for r in range(2)]
    for layer in range(layers):
        own = slice(layer % 2 * tile, (layer % 2 + 1) * tile)
        put(work, own, every, product(split(den[layer]), part(trans, mid, every)))
        spectrum = spectra[layer]
        for band in bands:
            out = product(part(basis, band, mid), part(work, own, every))
            for at in bands:
                term = spectrum * out[:, at]
                if layer == 0:
                    total[band, at] = term
                elif layer < layers - 1:
                    total[band, at] = total[band, at] + term
                else:
                    put(mixed, band, at, total[band, at] + term)

    def remote(number, src, dst, x, y):
        return pltpu.make_async_remote_copy(
            src_ref=src, dst_ref=dst, send_sem=send_sem.at[number], recv_sem=recv_sem.at[number],
            device_id={"gx": x, "gy": y}, device_id_type=MESH,
        )

    depth_of = RADIUS // CHUNKS

    def piece(rs, c):
        return slice(rs.start + c * depth_of, rs.start + (c + 1) * depth_of)

    beyond = {1: high, -1: low}
    near = {1: last, -1: first}
    far = {1: low, -1: high}
    lands = {1: first, -1: last}
    each = [(c, dx) for c in range(CHUNKS) for dx in steps]

    def numbered(kind, c, dx):
        return 3 + (kind * CHUNKS + c) * 2 + (dx < 0)

    def fold_core():
        return remote(0, big.at[edge, core_edge], from_c, gx, partner)

    def fold_partner():
        return remote(1, big.at[mid, core_edge], from_y.at[0], gx, partner)

    def fold_outer():
        return remote(2, big.at[mid, far_edge], from_y.at[1], gx, outer)

    def fold_x(c, dx):
        rs = slice(c * depth_of, (c + 1) * depth_of)
        return remote(numbered(0, c, dx), big.at[piece(beyond[dx], c), mid], from_x.at[int(dx < 0), rs], gx + dx, gy)

    def fold_d(c, dx):
        rs = slice(c * depth_of, (c + 1) * depth_of)
        return remote(numbered(1, c, dx), big.at[piece(beyond[dx], c), far_edge], from_d.at[int(dx < 0), rs], gx + dx, outer)

    def halo_partner(c, dx):
        rs = piece(lands[dx], c)
        return remote(numbered(5, c, dx), win.at[rs, core_near], win.at[rs, far_edge], gx, partner)

    def halo_outer(c, dx):
        rs = piece(lands[dx], c)
        return remote(numbered(6, c, dx), win.at[rs, far_near], win.at[rs, core_edge], gx, outer)

    def halo_x(c, dx):
        return remote(numbered(2, c, dx), win.at[piece(near[dx], c), mid], win.at[piece(far[dx], c), mid], gx + dx, gy)

    def halo_d(c, dx):
        return remote(numbered(3, c, dx), win.at[piece(near[dx], c), far_near], win.at[piece(far[dx], c), core_edge], gx + dx, outer)

    def halo_core(c, dx):
        return remote(numbered(4, c, dx), win.at[piece(far[dx], c), core_near], win.at[piece(far[dx], c), far_edge], gx, partner)

    def mix(cs):
        for band in bands:
            put(work, band, cs, product(part(mixed, band, every), part(basis, every, cs)))

    def back(rs, cs):
        big[rs, cs] = product(part(trans, rs, every), part(work, every, cs))

    for load in loads[layers + 6 : layers + 10]:
        load.wait()
    mix(edge)
    back(edge, edge)
    sides = 2 - (gx == 0).astype(jnp.int32) - (gx == nx - 1).astype(jnp.int32)
    pl.semaphore_wait(barrier, (sides + 1) * jnp.where(has_outer, 2, 1))
    fold_core().start()
    for c, dx in each:
        only_if(there(dx) & has_outer, lambda: fold_d(c, dx).start())
    mix(mid)
    back(edge, mid)
    fold_core().wait_recv()
    big[edge, core_near] = big[edge, core_near] + from_c[...]
    for c, dx in each:
        only_if(there(dx), lambda: fold_x(c, dx).start())
    back(mid, edge)
    back(mid, mid)
    fold_partner().start()
    only_if(has_outer, lambda: fold_outer().start())
    for load in loads[layers + 10 :]:
        load.wait()

    fold_partner().wait_recv()
    big[mid, core_near] = big[mid, core_near] + from_y[0]

    @pl.when(has_outer)
    def _():
        fold_outer().wait_recv()
        big[mid, far_near] = big[mid, far_near] + from_y[1]

    for c, dx in each:
        rs = piece(lands[dx], c)
        tile_rows = slice(rs.start - 2 * RADIUS, rs.stop - 2 * RADIUS)
        at = slice(c * depth_of, (c + 1) * depth_of)

        @pl.when(there(-dx))
        def _():
            fold_x(c, dx).wait_recv()
            big[rs, mid] = big[rs, mid] + from_x[int(dx < 0), at]

        @pl.when(there(-dx) & has_outer)
        def _():
            fold_d(c, dx).wait_recv()
            big[rs, far_near] = big[rs, far_near] + from_d[int(dx < 0), at]

        ahead = big[rs, mid]
        win[rs, mid] = sta[tile_rows, :].astype(F32) * (ahead - obs[tile_rows, :])
        only_if(there(-dx), lambda: halo_x(c, -dx).start())
        only_if(there(-dx) & has_outer, lambda: halo_d(c, -dx).start())
        halo_partner(c, dx).start()
        only_if(has_outer, lambda: halo_outer(c, dx).start())

    predicted[...] = big[mid, mid]
    residual[...] = win[mid, mid]

    for c, dx in each:
        halo_partner(c, dx).wait_recv()
        only_if(has_outer, lambda: halo_outer(c, dx).wait_recv())
    put(work, mid, every, product(split(win[mid, :]), part(trans, every, every)))
    for band in bands:
        total[band, :] = product(part(basis, band, mid), part(work, mid, every))

    fold_core().wait_send()
    fold_partner().wait_send()
    only_if(has_outer, lambda: fold_outer().wait_send())
    for c, dx in each:
        only_if(there(dx), lambda: fold_x(c, dx).wait_send())
        only_if(there(dx) & has_outer, lambda: fold_d(c, dx).wait_send())

    for c, dx in each:
        @pl.when(there(-dx))
        def _():
            halo_x(c, dx).wait_recv()
            halo_core(c, dx).start()

    wait_x[...] = product(split(win[edge, mid]), part(trans, mid, every))
    for c, dx in each:
        halo_partner(c, dx).wait_send()
        only_if(has_outer, lambda: halo_outer(c, dx).wait_send())
        only_if(there(dx), lambda: halo_x(c, dx).wait_send())
        only_if(there(dx) & has_outer, lambda: halo_d(c, dx).wait_send())

    for c, dx in each:
        only_if(there(-dx), lambda: halo_core(c, dx).wait_recv())
        only_if(there(-dx) & has_outer, lambda: halo_d(c, dx).wait_recv())
    put(work, edge, every, wait_x[...] + product(split(win[edge, edge]), part(trans, edge, every)))
    for band in bands:
        blocks[band, :] = total[band, :] + product(part(basis, band, edge), part(work, edge, every))

    for c, dx in each:
        only_if(there(-dx), lambda: halo_core(c, dx).wait_send())


def adjoint_kernel(
    predicted, residual, blocks, spectra, b_h, b_l, t_h, t_l,
    predicted_out, residual_out, gradient,
    z_h, z_l, w_h, w_l, grad, out_sem,
):
    layers, tile = spectra.shape[0], residual.shape[0]
    length = tile + 2 * RADIUS
    half = length // 2
    mid, every, own = slice(2 * RADIUS, length), slice(0, length), slice(0, tile)
    bands = [slice(r * half, (r + 1) * half) for r in range(2)]
    basis, trans = (b_h, b_l), (t_h, t_l)
    stores = [
        pltpu.make_async_copy(predicted, predicted_out, out_sem.at[0]),
        pltpu.make_async_copy(residual, residual_out, out_sem.at[1]),
    ]
    for store in stores:
        store.start()
    for layer in range(layers):
        spectrum = spectra[layer]
        mixed, work = (z_h.at[layer], z_l.at[layer]), (w_h.at[layer], w_l.at[layer])
        for band in bands:
            for at in bands:
                put(mixed, band, at, spectrum * blocks[band, at])
            put(work, band, own, product(part(mixed, band, every), part(basis, every, mid)))
    for layer in range(layers):
        work = (w_h.at[layer], w_l.at[layer])
        for n in range(2):
            rs = slice(n * RADIUS, (n + 1) * RADIUS)
            inner = slice(mid.start + n * RADIUS, mid.start + (n + 1) * RADIUS)
            grad[layer, rs] = product(part(trans, inner, every), part(work, every, own))
            store = pltpu.make_async_copy(grad.at[layer, rs], gradient.at[layer, rs], out_sem.at[2 + 2 * layer + n])
            store.start()
            stores.append(store)
    for store in stores:
        store.wait()


def solution(mesh):
    counts = (mesh.shape["gx"], mesh.shape["gy"])

    def body(density, observed, stations, layer_index):
        layers, tile = density.shape[0], density.shape[1]
        length = tile + 2 * RADIUS
        half = length // 2
        (bas_h, bas_l), (tra_h, tra_l), (cos_h, cos_l) = tables(length)
        anywhere = pl.BlockSpec(memory_space=pl.ANY)
        vmem = pl.BlockSpec(memory_space=pltpu.VMEM)
        big = pltpu.VMEM((length, length), F32)
        wide = pltpu.VMEM((length, length), BF16)
        small = pltpu.VMEM((half, half), BF16)
        predicted, residual, blocks, spectra, *kept = pl.pallas_call(
            functools.partial(forward_kernel, counts),
            out_shape=(
                pltpu.VMEM((tile, tile), F32),
                pltpu.VMEM((tile, tile), F32),
                pltpu.VMEM((length, length), F32),
                pltpu.VMEM((layers, half, half), F32),
                wide, wide, wide, wide,
            ),
            in_specs=[anywhere] * 10,
            out_specs=(vmem,) * 8,
            scratch_shapes=[
                pltpu.VMEM(density.shape, F32),
                pltpu.VMEM((tile, tile), F32),
                pltpu.VMEM((tile, tile), jnp.int32),
                small, small,
                wide, wide, wide, wide, big, big, big,
                pltpu.VMEM((2 * RADIUS, length), F32),
                pltpu.VMEM((2, RADIUS, tile), F32),
                pltpu.VMEM((2, tile, RADIUS), F32),
                pltpu.VMEM((2 * RADIUS, RADIUS), F32),
                pltpu.VMEM((2, RADIUS, RADIUS), F32),
                pltpu.SMEM((layers,), jnp.int32),
                pltpu.SemaphoreType.DMA,
                pltpu.SemaphoreType.DMA((layers + 12,)),
                pltpu.SemaphoreType.DMA((3 + 14 * CHUNKS,)),
                pltpu.SemaphoreType.DMA((3 + 14 * CHUNKS,)),
            ],
            compiler_params=pltpu.CompilerParams(
                collective_id=0, has_side_effects=True, vmem_limit_bytes=32 << 20
            ),
            name="forward",
        )(*map(in_hbm, (layer_index, density, observed, stations, bas_h, bas_l, tra_h, tra_l, cos_h, cos_l)))
        return pl.pallas_call(
            adjoint_kernel,
            out_shape=(
                jax.ShapeDtypeStruct((tile, tile), F32),
                jax.ShapeDtypeStruct((tile, tile), F32),
                jax.ShapeDtypeStruct((layers, tile, tile), F32),
            ),
            in_specs=[vmem] * 8,
            out_specs=(anywhere,) * 3,
            scratch_shapes=[
                pltpu.VMEM((layers, length, length), BF16),
                pltpu.VMEM((layers, length, length), BF16),
                pltpu.VMEM((layers, length, tile), BF16),
                pltpu.VMEM((layers, length, tile), BF16),
                pltpu.VMEM((layers, tile, tile), F32),
                pltpu.SemaphoreType.DMA((2 + 2 * layers,)),
            ],
            compiler_params=pltpu.CompilerParams(vmem_limit_bytes=24 << 20),
            name="adjoint",
        )(predicted, residual, blocks, spectra, *kept)

    in_specs = (P(None, "gx", "gy"), P("gx", "gy"), P("gx", "gy"), P())
    out_specs = (P("gx", "gy"), P("gx", "gy"), P(None, "gx", "gy"))
    return jax.shard_map(body, mesh=mesh, in_specs=in_specs, out_specs=out_specs, check_vma=False)
```
